256 devices in a mesh: shard: 16 (over x, y), replica: 16 (over z, core).
Axes of the slice: x: 4, y: 4, z: 8, core: 2. Of those that a mesh axis runs over, the one named last changes fastest.
Arguments:
- grads: bfloat16 [16, 18432, 1024], P('replica', 'shard')
- assignment: int32 [18], replicated, may hold values from 0 to 31, as said below
- piece_slot: int32 [18], replicated, may hold values from 0 to 17, each once
- left_roots: bfloat16 [32, 1024, 1024], P('shard')
- right_roots: bfloat16 [32, 1024, 1024], P('shard')
Outputs:
- statistics: float32 [32, 2, 1024, 1024], P('shard', None, 'replica')
- direction: bfloat16 [18432, 1024], P('shard')
The draws below stay inside these ranges and needn't reach their ends.
Inputs may be any that keep to these rules, and one draw needn't show every extreme that they name: `assignment`: values are distinct; in every draw some owner holds all 2 of its slots, and slot 31 is named. `piece_slot`: a permutation.
All inputs are finite; a program needn't handle non-finite values.
Results may differ from the reference program's by a relative error of at most 0.025.
Values may be sent and summed in bfloat16 or wider, within the bound.
No kernel may reach another device: no remote copies, remote signals or barrier semaphores. Data moves between devices by JAX's collectives and lax.ppermute only.
A program may use at most 128 MiB of HBM per device.

```python
import math
import jax
import jax.numpy as jnp
from jax import lax

B = 1024
SLOTS = 2
NB = 18
PR = 64
N_SHARD = 16
N_REPLICA = 16


def draw_grads(key, part):
    key = jax.random.fold_in(key, 11)
    key_noise, key_rows, key_cols = jax.random.split(key, 3)
    shape = (N_REPLICA, NB * B, B)
    row_scale = jnp.exp(jax.random.uniform(key_rows, (1, NB * B, 1), jnp.float32, 0.0, math.log(10.0)))
    col_scale = jnp.exp(jax.random.uniform(key_cols, (1, 1, B), jnp.float32, 0.0, math.log(10.0)))
    base = jax.random.normal(key_noise, shape, jnp.float32)
    return (base * row_scale * col_scale * 0.1).astype(jnp.bfloat16)


def draw_assignment(key, part):
    key = jax.random.fold_in(key, 5)
    key_owner, key_rest, key_order = jax.random.split(key, 3)
    total = N_SHARD * SLOTS
    top_slot = total - 1
    full_owner = jax.random.randint(key_owner, (), 0, N_SHARD - 1)
    first = full_owner * SLOTS + jnp.arange(SLOTS, dtype=jnp.int32)
    mixed = jax.random.permutation(key_rest, total).astype(jnp.int32)
    excluded = (mixed // SLOTS == full_owner) | (mixed == top_slot)
    order = jnp.argsort(excluded.astype(jnp.int32), stable=True)
    others = mixed[order]
    chosen = jnp.concatenate([first, jnp.full((1,), top_slot, jnp.int32), others])[:NB]
    return jax.random.permutation(key_order, chosen).astype(jnp.int32)


def root_blocks(key, spread):
    key_diag, key_off = jax.random.split(key)
    count = N_SHARD * SLOTS
    diagonal = jnp.exp(jax.random.uniform(key_diag, (count, B), jnp.float32, 0.0, math.log(2.5)))
    noise = jax.random.normal(key_off, (count, B, B), jnp.float32)
    symmetric = (noise + jnp.swapaxes(noise, 1, 2)) * (spread / math.sqrt(2.0 * B))
    identity = jnp.eye(B, dtype=jnp.float32)
    return (symmetric * (1.0 - identity) + identity * diagonal[:, :, None]).astype(jnp.bfloat16)


def draw_left_roots(key, part):
    key = jax.random.fold_in(key, 21)
    return root_blocks(key, 0.4)


def draw_right_roots(key, part):
    key = jax.random.fold_in(key, 37)
    return root_blocks(key, 0.4)


def setup_inputs(seed: int = 0) -> dict:
    key_of = jax.random.split(jax.random.key(seed), 6)
    grads = draw_grads(jax.random.fold_in(key_of[5], 71), 0)
    assignment = draw_assignment(jax.random.fold_in(key_of[5], 71), 0)
    piece_slot = jax.random.permutation(key_of[2], NB).astype(jnp.int32)
    left_roots = draw_left_roots(jax.random.fold_in(key_of[5], 71), 0)
    right_roots = draw_right_roots(jax.random.fold_in(key_of[5], 71), 0)
    return dict(grads=grads, assignment=assignment, piece_slot=piece_slot, left_roots=left_roots, right_roots=right_roots)


epsilon = 1e-06

def reference(grads, assignment, piece_slot, left_roots, right_roots):
    replicas = grads.shape[0]
    scale_gram = 1.0 / (B * N_REPLICA)
    layout = grads.reshape(replicas, N_SHARD, NB, PR, B)[:, :, piece_slot]
    blocks = jnp.transpose(layout, (2, 0, 1, 3, 4)).reshape(NB, replicas, B, B)
    left_sel = left_roots[assignment]
    right_sel = right_roots[assignment]

    def one_block(items):
        grad_set, left_root, right_root = items
        mean_block = (lax.optimization_barrier(jnp.sum(grad_set.astype(jnp.float32), 0)) / replicas).astype(jnp.bfloat16)

        def add_gram(carry, one_grad):
            left_term = jnp.dot(one_grad, one_grad.T, preferred_element_type=jnp.float32) * scale_gram
            right_term = jnp.dot(one_grad.T, one_grad, preferred_element_type=jnp.float32) * scale_gram
            stacked = lax.optimization_barrier(jnp.stack([left_term, right_term]).astype(jnp.bfloat16))
            return (carry + stacked.astype(jnp.float32), None)
        stats_block, unused = lax.scan(add_gram, jnp.zeros((2, B, B), jnp.float32), grad_set)
        left_applied = jnp.dot(left_root, mean_block, preferred_element_type=jnp.float32).astype(jnp.bfloat16)
        precond = jnp.dot(left_applied, right_root, preferred_element_type=jnp.float32).astype(jnp.bfloat16)
        pre_float = precond.astype(jnp.float32)
        grad_power = jnp.mean(jnp.square(mean_block.astype(jnp.float32)))
        pre_power = jnp.mean(jnp.square(pre_float))
        factor = jnp.sqrt((grad_power + epsilon) / (pre_power + epsilon))
        return (stats_block, (pre_float * factor).astype(jnp.bfloat16))
    stats_blocks, grafted = lax.map(one_block, (blocks, left_sel, right_sel))
    statistics = jnp.zeros((N_SHARD * SLOTS, 2, B, B), jnp.float32).at[assignment].set(stats_blocks)
    pieces = jnp.transpose(grafted.reshape(NB, N_SHARD, PR, B), (1, 0, 2, 3))
    direction = jnp.zeros_like(pieces).at[:, piece_slot].set(pieces).reshape(NB * B, B)
    return (statistics, direction)
```

```python
import functools

import jax
import jax.numpy as jnp
from jax import lax
from jax.experimental import pallas as pl
from jax.experimental.pallas import tpu as pltpu
from jax.sharding import Mesh, PartitionSpec as P

epsilon = 1e-06
f32 = jnp.float32
bf16 = jnp.bfloat16

SHARDS, DEPTH, CORES = 16, 8, 2
SLOTS, BLOCKS, ROWS, WIDTH = 2, 18, 64, 1024
HALF = BLOCKS // CORES
CHUNK = WIDTH // DEPTH

OWN, SEND, PLACE, KIND, OWNER, FILLED, SLOTKIND, PICK, SIZE = 0, 9, 18, 34, 52, 70, 72, 74, 128


def params(megabytes=40):
    return pltpu.CompilerParams(vmem_limit_bytes=megabytes * 1024 * 1024)


def cost(flops, moved):
    return pl.CostEstimate(flops=flops, bytes_accessed=moved, transcendentals=0)


def plan_body(assignment, piece_slot, table):
    shard, core = lax.axis_index("shard"), lax.axis_index("core")

    def clear(i, unused):
        table[i] = 0
        return unused

    lax.fori_loop(0, SIZE, clear, 0)

    def block(k, unused):
        slot, place = assignment[k], piece_slot[k]
        rank = jnp.int32(0)
        for other in range(BLOCKS):
            rank += jnp.where(assignment[other] < slot, 1, 0)
        kind, index = lax.rem(rank, CORES), lax.div(rank, CORES)
        owner, which = lax.div(slot, SLOTS), lax.rem(slot, SLOTS)
        table[jnp.where(kind == core, OWN, SEND) + index] = place
        table[KIND + place] = kind
        table[OWNER + place] = owner

        @pl.when(kind == core)
        def _():
            table[PLACE + owner] = index

        @pl.when(owner == shard)
        def _():
            table[FILLED + which] = 1
            table[SLOTKIND + which] = kind

        @pl.when((owner == shard) & (kind == core))
        def _():
            table[PICK] = which

        return unused

    lax.fori_loop(0, BLOCKS, block, 0)


def plan(assignment, piece_slot):
    smem = pl.BlockSpec(memory_space=pltpu.SMEM)
    return pl.pallas_call(
        plan_body,
        out_shape=jax.ShapeDtypeStruct((SIZE,), jnp.int32),
        in_specs=[smem, smem],
        out_specs=smem,
        name="plan",
    )(assignment, piece_slot)


def copy_all(copies):
    for copy in copies:
        copy.start()
    for copy in copies:
        copy.wait()


def swap_out_body(table, pieces, out, sems):
    copy_all([pltpu.make_async_copy(pieces.at[table[SEND + n]], out.at[n], sems.at[n]) for n in range(HALF)])


def route_out_body(table, pieces, other, out, sems):
    copies = []
    for owner in range(SHARDS):
        index = table[PLACE + owner]
        copies.append(pltpu.make_async_copy(pieces.at[table[OWN + index]], out.at[owner, 0], sems.at[2 * owner]))
        copies.append(pltpu.make_async_copy(other.at[index], out.at[owner, 1], sems.at[2 * owner + 1]))
    copy_all(copies)


def dma_call(body, count, shape, table, *arrays, name):
    size = 2 * shape[-1] * shape[-2] * count
    return pl.pallas_call(
        body,
        out_shape=jax.ShapeDtypeStruct(shape, bf16),
        in_specs=[pl.BlockSpec(memory_space=pltpu.SMEM)] + [pl.BlockSpec(memory_space=pl.ANY)] * len(arrays),
        out_specs=pl.BlockSpec(memory_space=pl.ANY),
        scratch_shapes=[pltpu.SemaphoreType.DMA((count,))],
        cost_estimate=cost(0, 2 * size),
        name=name,
    )(table, *arrays)


def pair_sum_body(table, mine, other, out):
    total = (mine[0].astype(f32) + other[0].astype(f32)).astype(bf16)
    for z in range(DEPTH):
        out[z, 0] = total[:, z * CHUNK : (z + 1) * CHUNK]


def pair_sum(table, pieces, other):
    return pl.pallas_call(
        pair_sum_body,
        out_shape=jax.ShapeDtypeStruct((DEPTH, HALF, ROWS, CHUNK), bf16),
        grid_spec=pltpu.PrefetchScalarGridSpec(
            num_scalar_prefetch=1,
            grid=(HALF,),
            in_specs=[
                pl.BlockSpec((1, ROWS, WIDTH), lambda n, table: (table[OWN + n], 0, 0)),
                pl.BlockSpec((1, ROWS, WIDTH), lambda n, table: (n, 0, 0)),
            ],
            out_specs=pl.BlockSpec((DEPTH, 1, ROWS, CHUNK), lambda n, table: (0, n, 0, 0)),
        ),
        cost_estimate=cost(HALF * ROWS * WIDTH, 6 * HALF * ROWS * WIDTH),
        name="pair_sum",
    )(table, pieces, other)


def mean_out_body(table, *refs):
    chunks, out = refs[:-1], refs[-1]
    me = lax.axis_index("z")

    def one(owner, unused):
        index = table[PLACE + owner]
        for shift in range(DEPTH):
            source = lax.rem(me + DEPTH - shift, DEPTH)
            columns = pl.ds(pl.multiple_of(source * CHUNK, CHUNK), CHUNK)
            mean = chunks[shift][index].astype(f32) * (1.0 / (DEPTH * CORES))
            out[owner, :, columns] = mean.astype(bf16)
        return unused

    lax.fori_loop(0, SHARDS, one, 0)


def mean_out(table, chunks):
    return pl.pallas_call(
        mean_out_body,
        out_shape=jax.ShapeDtypeStruct((SHARDS, ROWS, WIDTH), bf16),
        in_specs=[pl.BlockSpec(memory_space=pltpu.SMEM)] + [pl.BlockSpec(memory_space=pltpu.VMEM)] * DEPTH,
        out_specs=pl.BlockSpec(memory_space=pltpu.VMEM),
        compiler_params=params(),
        cost_estimate=cost(SHARDS * ROWS * WIDTH, 4 * SHARDS * ROWS * WIDTH),
        name="mean_out",
    )(table, *chunks)


STEPS = 4
STRIP = WIDTH // STEPS


def precond_body(table, mean, left, right, out, sums):
    step = pl.program_id(0)

    @pl.when(step == 0)
    def _():
        sums[...] = jnp.zeros_like(sums)

    rows = mean[pl.ds(pl.multiple_of(step * STRIP, STRIP), STRIP), :].astype(f32)
    sums[0:1, :] += jnp.sum(rows * rows, axis=0, keepdims=True)
    applied = jnp.dot(left[0], mean[...], preferred_element_type=f32).astype(bf16)
    strip = jnp.dot(applied, right[0], preferred_element_type=f32).astype(bf16)
    wide = strip.astype(f32)
    sums[1:2, :] += jnp.sum(wide * wide, axis=0, keepdims=True)
    group = STRIP // ROWS
    out[pl.ds(step * group, group)] = strip.reshape(group, ROWS, WIDTH)

    @pl.when(step == STEPS - 1)
    def _():
        grad_power = jnp.sum(sums[0:1, :], axis=1, keepdims=True) * (1.0 / (WIDTH * WIDTH))
        pre_power = jnp.sum(sums[1:2, :], axis=1, keepdims=True) * (1.0 / (WIDTH * WIDTH))
        factor = jnp.sqrt((grad_power + epsilon) / (pre_power + epsilon))

        def scale(i, unused):
            out[i] = (out[i].astype(f32) * factor).astype(bf16)
            return unused

        lax.fori_loop(0, SHARDS, scale, 0)


def precond(table, mean, left_roots, right_roots):
    return pl.pallas_call(
        precond_body,
        out_shape=jax.ShapeDtypeStruct((SHARDS, ROWS, WIDTH), bf16),
        grid_spec=pltpu.PrefetchScalarGridSpec(
            num_scalar_prefetch=1,
            grid=(STEPS,),
            in_specs=[
                pl.BlockSpec((WIDTH, WIDTH), lambda i, table: (0, 0)),
                pl.BlockSpec((1, STRIP, WIDTH), lambda i, table: (table[PICK], i, 0)),
                pl.BlockSpec((1, WIDTH, WIDTH), lambda i, table: (table[PICK], 0, 0)),
            ],
            out_specs=pl.BlockSpec((SHARDS, ROWS, WIDTH), lambda i, table: (0, 0, 0)),
            scratch_shapes=[pltpu.VMEM((8, WIDTH), f32)],
        ),
        compiler_params=params(),
        cost_estimate=cost(4 * WIDTH**3, 8 * WIDTH**2),
        name="precond",
    )(table, mean, left_roots, right_roots)


def gram_body(grads, out):
    step = pl.program_id(0)
    scale = 1.0 / (WIDTH * DEPTH * CORES)
    group = STRIP // ROWS
    strip = pl.ds(pl.multiple_of(step * STRIP, STRIP), STRIP)
    left = right = None
    for rep in range(CORES):
        whole = grads[:, rep].reshape(WIDTH, WIDTH)
        rows = grads[pl.ds(step * group, group), rep].reshape(STRIP, WIDTH)
        columns = grads[:, rep, :, strip].reshape(WIDTH, STRIP)
        first = lax.dot_general(rows, whole, (((1,), (1,)), ((), ())), preferred_element_type=f32)
        second = lax.dot_general(columns, whole, (((0,), (0,)), ((), ())), preferred_element_type=f32)
        left = first if left is None else left + first
        right = second if right is None else right + second
    per = STRIP // CHUNK
    out[:, 0] = (left * scale).astype(bf16).reshape(per, CHUNK, WIDTH)
    out[:, 1] = (right * scale).astype(bf16).reshape(per, CHUNK, WIDTH)


def gram(grads):
    per = STRIP // CHUNK
    return pl.pallas_call(
        gram_body,
        out_shape=jax.ShapeDtypeStruct((DEPTH, 2, CHUNK, WIDTH), bf16),
        grid=(STEPS,),
        in_specs=[pl.BlockSpec((SHARDS, CORES, ROWS, WIDTH), lambda i: (0, 0, 0, 0))],
        out_specs=pl.BlockSpec((per, 2, CHUNK, WIDTH), lambda i: (i, 0, 0, 0)),
        compiler_params=params(),
        cost_estimate=cost(8 * WIDTH**3, 8 * WIDTH**2),
        name="gram",
    )(grads)


def statistics_body(table, mine, other, out):
    core = lax.axis_index("core")
    rows = pl.ds(pl.multiple_of(core * ROWS, ROWS), ROWS)
    for slot in range(SLOTS):
        for side in range(2):
            kept = mine[side, rows, :].astype(f32)
            got = other[side].astype(f32)
            value = jnp.where(table[SLOTKIND + slot] == core, kept, got)
            out[slot, side] = jnp.where(table[FILLED + slot] == 1, value, 0.0)


def statistics_call(table, mine, other):
    vmem = pl.BlockSpec(memory_space=pltpu.VMEM)
    return pl.pallas_call(
        statistics_body,
        out_shape=jax.ShapeDtypeStruct((SLOTS, 2, ROWS, WIDTH), f32),
        in_specs=[pl.BlockSpec(memory_space=pltpu.SMEM), vmem, vmem],
        out_specs=vmem,
        compiler_params=params(),
        cost_estimate=cost(0, 14 * 2 * ROWS * WIDTH),
        name="statistics",
    )(table, mine, other)


def place_body(table, mine, other, out, sems):
    core = lax.axis_index("core")

    def each(act):
        for place in range(BLOCKS):
            kind, owner = table[KIND + place], table[OWNER + place]

            @pl.when(kind == core)
            def _():
                act(pltpu.make_async_copy(mine.at[owner], out.at[place], sems.at[place]))

            @pl.when(kind != core)
            def _():
                act(pltpu.make_async_copy(other.at[owner], out.at[place], sems.at[place]))

    each(lambda copy: copy.start())
    each(lambda copy: copy.wait())


def local(grads, assignment, piece_slot, left_roots, right_roots):
    core = lax.axis_index("core")
    swap = functools.partial(lax.ppermute, axis_name="core", perm=[(0, 1), (1, 0)])
    exchange = functools.partial(lax.all_to_all, axis_name="shard", split_axis=0, concat_axis=0, tiled=True)
    pieces = grads.reshape(BLOCKS, ROWS, WIDTH)
    table = plan(assignment, piece_slot)

    other = swap(dma_call(swap_out_body, HALF, (HALF, ROWS, WIDTH), table, pieces, name="swap_out"))

    routed = dma_call(
        route_out_body, 2 * SHARDS, (SHARDS, CORES, ROWS, WIDTH), table, pieces, other, name="route_out"
    )
    owned = exchange(routed)

    summed = pair_sum(table, pieces, other).reshape(DEPTH * HALF * ROWS, CHUNK)
    chunk = lax.psum_scatter(summed, "z", scatter_dimension=0, tiled=True)
    chunks = [chunk]
    for shift in range(1, DEPTH):
        chunks.append(lax.ppermute(chunk, "z", [(z, (z + shift) % DEPTH) for z in range(DEPTH)]))
    chunks = [part.reshape(HALF, ROWS, CHUNK) for part in chunks]
    mean = exchange(mean_out(table, chunks)).reshape(WIDTH, WIDTH)

    terms = gram(owned).reshape(DEPTH * 2 * CHUNK, WIDTH)
    share = lax.psum_scatter(terms, "z", scatter_dimension=0, tiled=True).reshape(2, CHUNK, WIDTH)
    other_share = swap(lax.dynamic_slice_in_dim(share, (1 - core) * ROWS, ROWS, 1))
    statistics = statistics_call(table, share, other_share)

    returned = exchange(precond(table, mean, left_roots, right_roots))
    direction = dma_call(
        place_body, BLOCKS, (BLOCKS, ROWS, WIDTH), table, returned, swap(returned), name="place"
    )
    return statistics, direction.reshape(BLOCKS * ROWS, WIDTH)


def solution(mesh):
    fine = Mesh(mesh.devices.reshape(SHARDS, DEPTH, CORES), ("shard", "z", "core"))
    roots = P("shard", None, None)
    return jax.shard_map(
        local,
        mesh=fine,
        in_specs=(P(("z", "core"), "shard", None), P(), P(), roots, roots),
        out_specs=(P("shard", None, ("z", "core"), None), P("shard", None)),
        check_vma=False,
    )
```

```python
import functools

import jax
import jax.numpy as jnp
from jax import lax
from jax.experimental import pallas as pl
from jax.experimental.pallas import tpu as pltpu
from jax.sharding import Mesh, PartitionSpec as P

epsilon = 1e-06
f32 = jnp.float32
bf16 = jnp.bfloat16

SHARDS, DEPTH, CORES = 16, 8, 2
SLOTS, BLOCKS, ROWS, WIDTH = 2, 18, 64, 1024
HALF = BLOCKS // CORES
CHUNK = WIDTH // DEPTH

OWN, SEND, PLACE, KIND, OWNER, FILLED, SLOTKIND, PICK, USED, SIZE = 0, 9, 18, 34, 52, 70, 72, 74, 75, 128


def params(megabytes=32):
    return pltpu.CompilerParams(vmem_limit_bytes=megabytes * 1024 * 1024)


def cost(flops, moved):
    return pl.CostEstimate(flops=flops, bytes_accessed=moved, transcendentals=0)


def front_body(assignment, piece_slot, pieces, table, out, held, sem):
    shard, core = lax.axis_index("shard"), lax.axis_index("core")
    fetch = pltpu.make_async_copy(pieces, held, sem)
    fetch.start()

    def clear(i, unused):
        table[i] = 0
        return unused

    lax.fori_loop(0, USED, clear, 0)

    def block(k, unused):
        slot, place = assignment[k], piece_slot[k]
        rank = jnp.int32(0)
        for other in range(BLOCKS):
            rank += jnp.where(assignment[other] < slot, 1, 0)
        kind, index = lax.rem(rank, CORES), lax.div(rank, CORES)
        owner, which = lax.div(slot, SLOTS), lax.rem(slot, SLOTS)
        table[jnp.where(kind == core, OWN, SEND) + index] = place
        table[KIND + place] = kind
        table[OWNER + place] = owner

        @pl.when(kind == core)
        def _():
            table[PLACE + owner] = index

        @pl.when(owner == shard)
        def _():
            table[FILLED + which] = 1
            table[SLOTKIND + which] = kind

        @pl.when((owner == shard) & (kind == core))
        def _():
            table[PICK] = which

        return unused

    lax.fori_loop(0, BLOCKS, block, 0)
    fetch.wait()
    for n in range(HALF):
        out[n] = held[table[SEND + n]]


def front(assignment, piece_slot, pieces):
    smem = pl.BlockSpec(memory_space=pltpu.SMEM)
    return pl.pallas_call(
        front_body,
        out_shape=(
            jax.ShapeDtypeStruct((SIZE,), jnp.int32),
            jax.ShapeDtypeStruct((HALF, ROWS, WIDTH), bf16),
        ),
        in_specs=[smem, smem, pl.BlockSpec(memory_space=pl.ANY)],
        out_specs=(smem, pl.BlockSpec(memory_space=pltpu.VMEM)),
        scratch_shapes=[pltpu.VMEM((BLOCKS, ROWS, WIDTH), bf16), pltpu.SemaphoreType.DMA],
        compiler_params=params(56),
        cost_estimate=cost(0, 6 * BLOCKS * ROWS * WIDTH),
        name="front",
    )(assignment, piece_slot, pieces)


TEAM = 4


def route_body(table, pieces, other, routed, *rest):
    sums, held = rest[:-1], rest[-1]
    step = pl.program_id(0)
    me = lax.axis_index("z")
    for i in range(TEAM):
        index = table[PLACE + TEAM * step + i]
        routed[i, 0] = pieces[table[OWN + index]]
        routed[i, 1] = other[index]

    def add(n):
        held[...] = (pieces[table[OWN + n]].astype(f32) + other[n].astype(f32)).astype(bf16)
        for shift in range(DEPTH):
            target = lax.rem(me + shift, DEPTH)
            sums[shift][n] = held[:, pl.ds(pl.multiple_of(target * CHUNK, CHUNK), CHUNK)]

    for i in range(2):
        add(2 * step + i)

    @pl.when(step == SHARDS // TEAM - 1)
    def _():
        add(HALF - 1)


def route(table, pieces, other):
    chunk = jax.ShapeDtypeStruct((HALF, ROWS, CHUNK), bf16)
    chunk_spec = pl.BlockSpec((HALF, ROWS, CHUNK), lambda i, table: (0, 0, 0))
    routed, *sums = pl.pallas_call(
        route_body,
        out_shape=(pltpu.HBM((SHARDS, CORES, ROWS, WIDTH), bf16), *[chunk] * DEPTH),
        grid_spec=pltpu.PrefetchScalarGridSpec(
            num_scalar_prefetch=1,
            grid=(SHARDS // TEAM,),
            in_specs=[
                pl.BlockSpec((BLOCKS, ROWS, WIDTH), lambda i, table: (0, 0, 0)),
                pl.BlockSpec((HALF, ROWS, WIDTH), lambda i, table: (0, 0, 0)),
            ],
            out_specs=(
                pl.BlockSpec((TEAM, CORES, ROWS, WIDTH), lambda i, table: (i, 0, 0, 0)),
                *[chunk_spec] * DEPTH,
            ),
            scratch_shapes=[pltpu.VMEM((ROWS, WIDTH), bf16)],
        ),
        compiler_params=params(),
        cost_estimate=cost(0, 16 * SHARDS * ROWS * WIDTH),
        name="route",
    )(table, pieces, other)
    return routed, sums


def mean_body(*refs):
    parts, out = refs[:-1], refs[-1]
    for n in range(HALF):
        total = parts[0][n].astype(f32)
        for part in parts[1:]:
            total += part[n].astype(f32)
        out[n] = (total * (1.0 / (DEPTH * CORES))).astype(bf16)


def mean_of(parts):
    vmem = pl.BlockSpec(memory_space=pltpu.VMEM)
    return pl.pallas_call(
        mean_body,
        out_shape=jax.ShapeDtypeStruct((HALF, ROWS, CHUNK), bf16),
        in_specs=[vmem] * DEPTH,
        out_specs=vmem,
        compiler_params=params(),
        cost_estimate=cost(DEPTH * HALF * ROWS * CHUNK, 18 * HALF * ROWS * CHUNK),
        name="mean",
    )(*parts)


def mean_out_body(table, *refs):
    chunks, out = refs[:-1], refs[-1]
    me = lax.axis_index("z")

    def one(owner, unused):
        index = table[PLACE + owner]
        for shift in range(DEPTH):
            source = lax.rem(me + DEPTH - shift, DEPTH)
            columns = pl.ds(pl.multiple_of(source * CHUNK, CHUNK), CHUNK)
            out[owner, :, columns] = chunks[shift][index]
        return unused

    lax.fori_loop(0, SHARDS, one, 0)


def mean_out(table, chunks):
    return pl.pallas_call(
        mean_out_body,
        out_shape=pltpu.HBM((SHARDS, ROWS, WIDTH), bf16),
        in_specs=[pl.BlockSpec(memory_space=pltpu.SMEM)] + [pl.BlockSpec(memory_space=pltpu.VMEM)] * DEPTH,
        out_specs=pl.BlockSpec((SHARDS, ROWS, WIDTH), lambda: (0, 0, 0)),
        compiler_params=params(),
        cost_estimate=cost(0, 4 * SHARDS * ROWS * WIDTH),
        name="mean_out",
    )(table, *chunks)


def pick_body(table, left, right, out, sems):
    slot = table[PICK]
    copies = [
        pltpu.make_async_copy(left.at[slot], out.at[0], sems.at[0]),
        pltpu.make_async_copy(right.at[slot], out.at[1], sems.at[1]),
    ]
    for copy in copies:
        copy.start()
    for copy in copies:
        copy.wait()


def pick(table, left_roots, right_roots):
    return pl.pallas_call(
        pick_body,
        out_shape=pltpu.VMEM((2, WIDTH, WIDTH), bf16),
        in_specs=[pl.BlockSpec(memory_space=pltpu.SMEM)] + [pl.BlockSpec(memory_space=pl.ANY)] * 2,
        out_specs=pl.BlockSpec(memory_space=pltpu.VMEM),
        scratch_shapes=[pltpu.SemaphoreType.DMA((2,))],
        compiler_params=params(),
        cost_estimate=cost(0, 8 * WIDTH**2),
        name="pick",
    )(table, left_roots, right_roots)


STEPS = 4
STRIP = WIDTH // STEPS


def precond_body(mean, roots, out, sums, scaled):
    sums[...] = jnp.zeros_like(sums)
    group = STRIP // ROWS

    def strip(step, unused):
        rows = pl.ds(pl.multiple_of(step * STRIP, STRIP), STRIP)
        own = mean[rows, :].astype(f32)
        sums[0:1, :] += jnp.sum(own * own, axis=0, keepdims=True)
        applied = jnp.dot(roots[0, rows, :], mean[...], preferred_element_type=f32).astype(bf16)
        product = jnp.dot(applied, roots[1], preferred_element_type=f32).astype(bf16)
        wide = product.astype(f32)
        sums[1:2, :] += jnp.sum(wide * wide, axis=0, keepdims=True)
        scaled[pl.ds(step * group, group)] = product.reshape(group, ROWS, WIDTH)
        return unused

    lax.fori_loop(0, STEPS, strip, 0)
    grad_power = jnp.sum(sums[0:1, :], axis=1, keepdims=True) * (1.0 / (WIDTH * WIDTH))
    pre_power = jnp.sum(sums[1:2, :], axis=1, keepdims=True) * (1.0 / (WIDTH * WIDTH))
    factor = jnp.sqrt((grad_power + epsilon) / (pre_power + epsilon))

    def scale(i, unused):
        out[i] = (scaled[i].astype(f32) * factor).astype(bf16)
        return unused

    lax.fori_loop(0, SHARDS, scale, 0)


def precond(mean, roots):
    vmem = pl.BlockSpec(memory_space=pltpu.VMEM)
    return pl.pallas_call(
        precond_body,
        out_shape=jax.ShapeDtypeStruct((SHARDS, ROWS, WIDTH), bf16),
        in_specs=[vmem, vmem],
        out_specs=vmem,
        scratch_shapes=[pltpu.VMEM((8, WIDTH), f32), pltpu.VMEM((SHARDS, ROWS, WIDTH), bf16)],
        compiler_params=params(),
        cost_estimate=cost(80 * WIDTH**3, 8 * WIDTH**2),
        name="precond",
    )(mean, roots)


def gram_body(grads, out):
    step = pl.program_id(0)
    scale = 1.0 / (WIDTH * DEPTH * CORES)
    group = STRIP // ROWS
    strip = pl.ds(pl.multiple_of(step * STRIP, STRIP), STRIP)
    left = right = None
    for rep in range(CORES):
        whole = grads[:, rep].reshape(WIDTH, WIDTH)
        rows = grads[pl.ds(step * group, group), rep].reshape(STRIP, WIDTH)
        columns = grads[:, rep, :, strip].reshape(WIDTH, STRIP)
        first = lax.dot_general(rows, whole, (((1,), (1,)), ((), ())), preferred_element_type=f32)
        second = lax.dot_general(columns, whole, (((0,), (0,)), ((), ())), preferred_element_type=f32)
        left = first if left is None else left + first
        right = second if right is None else right + second
    per = STRIP // CHUNK
    out[:, 0] = (left * scale).astype(bf16).reshape(per, CHUNK, WIDTH)
    out[:, 1] = (right * scale).astype(bf16).reshape(per, CHUNK, WIDTH)


def gram(grads):
    per = STRIP // CHUNK
    return pl.pallas_call(
        gram_body,
        out_shape=pltpu.HBM((DEPTH, 2, CHUNK, WIDTH), bf16),
        grid=(STEPS,),
        in_specs=[pl.BlockSpec((SHARDS, CORES, ROWS, WIDTH), lambda i: (0, 0, 0, 0))],
        out_specs=pl.BlockSpec((per, 2, CHUNK, WIDTH), lambda i: (i, 0, 0, 0)),
        compiler_params=params(),
        cost_estimate=cost(8 * WIDTH**3, 8 * WIDTH**2),
        name="gram",
    )(grads)


def statistics_body(table, mine, other, out):
    core = lax.axis_index("core")
    rows = pl.ds(pl.multiple_of(core * ROWS, ROWS), ROWS)
    for slot in range(SLOTS):
        for side in range(2):
            kept = mine[side, rows, :].astype(f32)
            got = other[side, rows, :].astype(f32)
            value = jnp.where(table[SLOTKIND + slot] == core, kept, got)
            out[slot, side] = jnp.where(table[FILLED + slot] == 1, value, 0.0)


def statistics_call(table, mine, other):
    vmem = pl.BlockSpec(memory_space=pltpu.VMEM)
    return pl.pallas_call(
        statistics_body,
        out_shape=jax.ShapeDtypeStruct((SLOTS, 2, ROWS, WIDTH), f32),
        in_specs=[pl.BlockSpec(memory_space=pltpu.SMEM), vmem, vmem],
        out_specs=vmem,
        compiler_params=params(),
        cost_estimate=cost(0, 14 * 2 * ROWS * WIDTH),
        name="statistics",
    )(table, mine, other)


GROUP = 6


def place_body(table, mine, other, out):
    core = lax.axis_index("core")
    step = pl.program_id(0)
    for i in range(GROUP):
        kind, owner = table[KIND + GROUP * step + i], table[OWNER + GROUP * step + i]

        @pl.when(kind == core)
        def _():
            out[i] = mine[owner]

        @pl.when(kind != core)
        def _():
            out[i] = other[owner]


def place(table, mine, other):
    whole = pl.BlockSpec(memory_space=pltpu.VMEM)
    return pl.pallas_call(
        place_body,
        out_shape=jax.ShapeDtypeStruct((BLOCKS, ROWS, WIDTH), bf16),
        grid_spec=pltpu.PrefetchScalarGridSpec(
            num_scalar_prefetch=1,
            grid=(BLOCKS // GROUP,),
            in_specs=[whole, whole],
            out_specs=pl.BlockSpec((GROUP, ROWS, WIDTH), lambda i, table: (i, 0, 0)),
        ),
        compiler_params=params(),
        cost_estimate=cost(0, 4 * BLOCKS * ROWS * WIDTH),
        name="place",
    )(table, mine, other)


def local(grads, assignment, piece_slot, left_roots, right_roots):
    swap = functools.partial(lax.ppermute, axis_name="core", perm=[(0, 1), (1, 0)])
    exchange = functools.partial(lax.all_to_all, axis_name="shard", split_axis=0, concat_axis=0, tiled=True)

    def along(array, shift):
        return lax.ppermute(array, "z", [(z, (z + shift) % DEPTH) for z in range(DEPTH)])

    pieces = grads.reshape(BLOCKS, ROWS, WIDTH)
    table, outgoing = front(assignment, piece_slot, pieces)
    other = swap(outgoing)

    routed, sums = route(table, pieces, other)
    owned = exchange(routed)
    chunk = mean_of([sums[0]] + [along(sums[shift], shift) for shift in range(1, DEPTH)])
    chunks = [chunk] + [along(chunk, shift) for shift in range(1, DEPTH)]
    roots = pick(table, left_roots, right_roots)
    owned, roots, *chunks = lax.optimization_barrier((owned, roots, *chunks))
    packed, owned = lax.optimization_barrier((mean_out(table, chunks), owned))
    mean = exchange(packed).reshape(WIDTH, WIDTH)

    terms = gram(owned)
    mean, unused = lax.optimization_barrier((mean, terms))
    share = lax.psum_scatter(terms.reshape(DEPTH * 2 * CHUNK, WIDTH), "z", scatter_dimension=0, tiled=True)
    share = share.reshape(2, CHUNK, WIDTH)
    statistics = statistics_call(table, share, swap(share))

    returned = exchange(precond(mean, roots))
    returned, statistics = lax.optimization_barrier((returned, statistics))
    direction = place(table, returned, swap(returned))
    return statistics, direction.reshape(BLOCKS * ROWS, WIDTH)


def solution(mesh):
    fine = Mesh(mesh.devices.reshape(SHARDS, DEPTH, CORES), ("shard", "z", "core"))
    roots = P("shard", None, None)
    return jax.shard_map(
        local,
        mesh=fine,
        in_specs=(P(("z", "core"), "shard", None), P(), P(), roots, roots),
        out_specs=(P("shard", None, ("z", "core"), None), P("shard", None)),
        check_vma=False,
    )
```

```python
import functools

import jax
import jax.numpy as jnp
from jax import lax
from jax.experimental import pallas as pl
from jax.experimental.pallas import tpu as pltpu
from jax.sharding import Mesh, PartitionSpec as P

epsilon = 1e-06
f32 = jnp.float32
bf16 = jnp.bfloat16

SHARDS, DEPTH, CORES = 16, 8, 2
SLOTS, BLOCKS, ROWS, WIDTH = 2, 18, 64, 1024
HALF = BLOCKS // CORES
CHUNK = WIDTH // DEPTH

ORDER = (4, 3, 5, 2, 6, 1, 7)

OWN, SEND, PLACE, KIND, OWNER, FILLED, SLOTKIND, PICK, USED, SIZE = 0, 9, 18, 34, 52, 70, 72, 74, 75, 128


def params(megabytes=32):
    return pltpu.CompilerParams(vmem_limit_bytes=megabytes * 1024 * 1024)


def cost(flops, moved):
    return pl.CostEstimate(flops=flops, bytes_accessed=moved, transcendentals=0)


def front_body(assignment, piece_slot, pieces, table, out, held, sem):
    shard, core = lax.axis_index("shard"), lax.axis_index("core")
    fetch = pltpu.make_async_copy(pieces, held, sem)
    fetch.start()

    def clear(i, unused):
        table[i] = 0
        return unused

    lax.fori_loop(0, USED, clear, 0)

    def block(k, unused):
        slot, place = assignment[k], piece_slot[k]
        rank = jnp.int32(0)
        for other in range(BLOCKS):
            rank += jnp.where(assignment[other] < slot, 1, 0)
        kind, index = lax.rem(rank, CORES), lax.div(rank, CORES)
        owner, which = lax.div(slot, SLOTS), lax.rem(slot, SLOTS)
        table[jnp.where(kind == core, OWN, SEND) + index] = place
        table[KIND + place] = kind
        table[OWNER + place] = owner

        @pl.when(kind == core)
        def _():
            table[PLACE + owner] = index

        @pl.when(owner == shard)
        def _():
            table[FILLED + which] = 1
            table[SLOTKIND + which] = kind

        @pl.when((owner == shard) & (kind == core))
        def _():
            table[PICK] = which

        return unused

    lax.fori_loop(0, BLOCKS, block, 0)
    fetch.wait()
    for n in range(HALF):
        out[n] = held[table[SEND + n]]


def front(assignment, piece_slot, pieces):
    smem = pl.BlockSpec(memory_space=pltpu.SMEM)
    return pl.pallas_call(
        front_body,
        out_shape=(
            pltpu.HBM((SIZE,), jnp.int32),
            jax.ShapeDtypeStruct((HALF, ROWS, WIDTH), bf16),
        ),
        in_specs=[smem, smem, pl.BlockSpec(memory_space=pl.ANY)],
        out_specs=(smem, pl.BlockSpec(memory_space=pltpu.VMEM)),
        scratch_shapes=[pltpu.VMEM((BLOCKS, ROWS, WIDTH), bf16), pltpu.SemaphoreType.DMA],
        compiler_params=params(56),
        cost_estimate=cost(0, 6 * BLOCKS * ROWS * WIDTH),
        name="front",
    )(assignment, piece_slot, pieces)


def pair_sum_body(table, pieces, other, *rest):
    sums, held = rest[:-1], rest[-1]
    me = lax.axis_index("z")

    def add(n, unused):
        held[...] = (pieces[table[OWN + n]].astype(f32) + other[n].astype(f32)).astype(bf16)
        for shift in range(DEPTH):
            target = lax.rem(me + shift, DEPTH)
            sums[shift][n] = held[:, pl.ds(pl.multiple_of(target * CHUNK, CHUNK), CHUNK)]
        return unused

    lax.fori_loop(0, HALF, add, 0)


def pair_sum(table, pieces, other):
    vmem = pl.BlockSpec(memory_space=pltpu.VMEM)
    return pl.pallas_call(
        pair_sum_body,
        out_shape=[jax.ShapeDtypeStruct((HALF, ROWS, CHUNK), bf16)] * DEPTH,
        in_specs=[pl.BlockSpec(memory_space=pltpu.SMEM), vmem, vmem],
        out_specs=[vmem] * DEPTH,
        scratch_shapes=[pltpu.VMEM((ROWS, WIDTH), bf16)],
        compiler_params=params(),
        cost_estimate=cost(HALF * ROWS * WIDTH, 6 * HALF * ROWS * WIDTH),
        name="pair_sum",
    )(table, pieces, other)


TEAM = 4


def route_own_body(table, pieces, routed):
    step = pl.program_id(0)
    for i in range(TEAM):
        routed[i, 0] = pieces[table[OWN + table[PLACE + TEAM * step + i]]]


def route_other_body(table, other, half, routed):
    step = pl.program_id(0)
    for i in range(TEAM):
        routed[i, 0] = other[table[PLACE + TEAM * step + i]]


def route(table, source, half=None):
    part = 0 if half is None else 1
    block = pl.BlockSpec((TEAM, 1, ROWS, WIDTH), lambda i, table: (i, part, 0, 0))
    return pl.pallas_call(
        route_other_body if part else route_own_body,
        out_shape=pltpu.HBM((SHARDS, CORES, ROWS, WIDTH), bf16),
        grid_spec=pltpu.PrefetchScalarGridSpec(
            num_scalar_prefetch=1,
            grid=(SHARDS // TEAM,),
            in_specs=[pl.BlockSpec(memory_space=pltpu.VMEM)] + [pl.BlockSpec(memory_space=pl.ANY)] * part,
            out_specs=block,
        ),
        input_output_aliases={2: 0} if part else {},
        compiler_params=params(),
        cost_estimate=cost(0, 4 * SHARDS * ROWS * WIDTH),
        name="route_other" if part else "route_own",
    )(table, source, *([half] if part else []))


def mean_body(*refs):
    parts, out = refs[:-1], refs[-1]
    for n in range(HALF):
        total = parts[0][n].astype(f32)
        for part in parts[1:]:
            total += part[n].astype(f32)
        out[n] = (total * (1.0 / (DEPTH * CORES))).astype(bf16)


def mean_of(parts):
    vmem = pl.BlockSpec(memory_space=pltpu.VMEM)
    return pl.pallas_call(
        mean_body,
        out_shape=jax.ShapeDtypeStruct((HALF, ROWS, CHUNK), bf16),
        in_specs=[vmem] * DEPTH,
        out_specs=vmem,
        compiler_params=params(),
        cost_estimate=cost(DEPTH * HALF * ROWS * CHUNK, 18 * HALF * ROWS * CHUNK),
        name="mean",
    )(*parts)


def mean_out_body(table, *refs):
    chunks, out = refs[:-1], refs[-1]
    me, step = lax.axis_index("z"), pl.program_id(0)

    def one(i, unused):
        index = table[PLACE + TEAM * step + i]
        for chunk, shift in zip(chunks, (*reversed(ORDER), 0)):
            source = lax.rem(me + DEPTH - shift, DEPTH)
            columns = pl.ds(pl.multiple_of(source * CHUNK, CHUNK), CHUNK)
            out[i, :, columns] = chunk[index]
        return unused

    lax.fori_loop(0, TEAM, one, 0)


def mean_out(table, chunks):
    return pl.pallas_call(
        mean_out_body,
        out_shape=pltpu.HBM((SHARDS, ROWS, WIDTH), bf16),
        grid_spec=pltpu.PrefetchScalarGridSpec(
            num_scalar_prefetch=1,
            grid=(SHARDS // TEAM,),
            in_specs=[pl.BlockSpec(memory_space=pltpu.VMEM)] * DEPTH,
            out_specs=pl.BlockSpec((TEAM, ROWS, WIDTH), lambda i, table: (i, 0, 0)),
        ),
        compiler_params=params(),
        cost_estimate=cost(0, 4 * SHARDS * ROWS * WIDTH),
        name="mean_out",
    )(table, *chunks)


STEPS = 4
STRIP = WIDTH // STEPS
LONG = WIDTH // 2


def precond_body(table, mean, left, right, out, roots, middle, scaled, sums, sems):
    slot = table[PICK]
    second = pltpu.make_async_copy(right.at[slot], roots.at[1], sems.at[STEPS])
    first = pltpu.make_async_copy(left.at[slot], roots.at[0], sems.at[STEPS + 1])
    second.start()
    first.start()
    sums[...] = jnp.zeros_like(sums)
    group = LONG // ROWS

    def power(step, unused):
        own = mean[pl.ds(pl.multiple_of(step * STRIP, STRIP), STRIP), :].astype(f32)
        sums[0:1, :] += jnp.sum(own * own, axis=0, keepdims=True)
        return unused

    lax.fori_loop(0, STEPS, power, 0)
    second.wait()

    def apply_right(step, unused):
        rows = pl.ds(pl.multiple_of(step * LONG, LONG), LONG)
        middle[rows, :] = jnp.dot(mean[rows, :], roots[1], preferred_element_type=f32).astype(bf16)
        return unused

    lax.fori_loop(0, WIDTH // LONG, apply_right, 0)
    first.wait()

    def apply_left(step, unused):
        rows = pl.ds(pl.multiple_of(step * LONG, LONG), LONG)
        product = jnp.dot(roots[0, rows, :], middle[...], preferred_element_type=f32).astype(bf16)
        wide = product.astype(f32)
        sums[1:2, :] += jnp.sum(wide * wide, axis=0, keepdims=True)
        scaled[pl.ds(step * group, group)] = product.reshape(group, ROWS, WIDTH)
        return unused

    lax.fori_loop(0, WIDTH // LONG, apply_left, 0)
    grad_power = jnp.sum(sums[0:1, :], axis=1, keepdims=True) * (1.0 / (WIDTH * WIDTH))
    pre_power = jnp.sum(sums[1:2, :], axis=1, keepdims=True) * (1.0 / (WIDTH * WIDTH))
    factor = jnp.sqrt((grad_power + epsilon) / (pre_power + epsilon))
    sends = []
    for step in range(STEPS):
        part = pl.ds(step * TEAM, TEAM)

        def scale(i, unused, step=step):
            scaled[step * TEAM + i] = (scaled[step * TEAM + i].astype(f32) * factor).astype(bf16)
            return unused

        lax.fori_loop(0, TEAM, scale, 0)
        sends.append(pltpu.make_async_copy(scaled.at[part], out.at[part], sems.at[step]))
        sends[-1].start()
    for send in sends:
        send.wait()


def precond(table, mean, left_roots, right_roots):
    anywhere = pl.BlockSpec(memory_space=pl.ANY)
    left_roots = pltpu.with_memory_space_constraint(left_roots, pltpu.HBM)
    right_roots = pltpu.with_memory_space_constraint(right_roots, pltpu.HBM)
    return pl.pallas_call(
        precond_body,
        out_shape=pltpu.HBM((SHARDS, ROWS, WIDTH), bf16),
        in_specs=[
            pl.BlockSpec(memory_space=pltpu.SMEM),
            pl.BlockSpec(memory_space=pltpu.VMEM),
            anywhere,
            anywhere,
        ],
        out_specs=anywhere,
        scratch_shapes=[
            pltpu.VMEM((2, WIDTH, WIDTH), bf16),
            pltpu.VMEM((WIDTH, WIDTH), bf16),
            pltpu.VMEM((SHARDS, ROWS, WIDTH), bf16),
            pltpu.VMEM((8, WIDTH), f32),
            pltpu.SemaphoreType.DMA((STEPS + 2,)),
        ],
        compiler_params=params(),
        cost_estimate=cost(80 * WIDTH**3, 8 * WIDTH**2),
        name="precond",
    )(table, mean, left_roots, right_roots)


def gram_body(grads, out, whole, terms, sems):
    scale = 1.0 / (WIDTH * DEPTH * CORES)
    per = STRIP // CHUNK
    for rep in range(CORES):
        whole[rep] = grads[:, rep].reshape(WIDTH, WIDTH)
    sends = []
    for step in range(STEPS):
        here = slice(step * STRIP, (step + 1) * STRIP)
        rest = slice(step * STRIP, WIDTH)
        left = right = None
        for rep in range(CORES):
            first = lax.dot_general(
                whole[rep, here, :], whole[rep, rest, :], (((1,), (1,)), ((), ())), preferred_element_type=f32
            )
            second = lax.dot_general(
                whole[rep, :, here], whole[rep, :, rest], (((0,), (0,)), ((), ())), preferred_element_type=f32
            )
            left = first if left is None else left + first
            right = second if right is None else right + second
        for side, value in enumerate((left, right)):
            value = value * scale
            terms[step * per : (step + 1) * per, side, :, rest] = value.astype(bf16).reshape(per, CHUNK, -1)
            for other in range(step + 1, STEPS):
                offset = (other - step) * STRIP
                cell = value[:, offset : offset + STRIP].T.astype(bf16).reshape(per, CHUNK, STRIP)
                terms[other * per : (other + 1) * per, side, :, here] = cell
        part = pl.ds(step * per, per)
        sends.append(pltpu.make_async_copy(terms.at[part], out.at[part], sems.at[step]))
        sends[-1].start()
    for send in sends:
        send.wait()


def gram(grads):
    return pl.pallas_call(
        gram_body,
        out_shape=pltpu.HBM((DEPTH, 2, CHUNK, WIDTH), bf16),
        in_specs=[pl.BlockSpec(memory_space=pltpu.VMEM)],
        out_specs=pl.BlockSpec(memory_space=pl.ANY),
        scratch_shapes=[
            pltpu.VMEM((CORES, WIDTH, WIDTH), bf16),
            pltpu.VMEM((DEPTH, 2, CHUNK, WIDTH), bf16),
            pltpu.SemaphoreType.DMA((STEPS,)),
        ],
        compiler_params=params(),
        cost_estimate=cost(8 * WIDTH**3, 8 * WIDTH**2),
        name="gram",
    )(grads)


def statistics_body(table, mine, other, out):
    core = lax.axis_index("core")
    rows = pl.ds(pl.multiple_of(core * ROWS, ROWS), ROWS)
    for slot in range(SLOTS):
        for side in range(2):
            kept = mine[side, rows, :].astype(f32)
            got = other[side, rows, :].astype(f32)
            value = jnp.where(table[SLOTKIND + slot] == core, kept, got)
            out[slot, side] = jnp.where(table[FILLED + slot] == 1, value, 0.0)


def statistics_call(table, mine, other):
    vmem = pl.BlockSpec(memory_space=pltpu.VMEM)
    return pl.pallas_call(
        statistics_body,
        out_shape=jax.ShapeDtypeStruct((SLOTS, 2, ROWS, WIDTH), f32),
        in_specs=[pl.BlockSpec(memory_space=pltpu.SMEM), vmem, vmem],
        out_specs=vmem,
        compiler_params=params(),
        cost_estimate=cost(0, 14 * 2 * ROWS * WIDTH),
        name="statistics",
    )(table, mine, other)


GROUP = 6


def place_body(table, mine, other, out):
    core = lax.axis_index("core")
    step = pl.program_id(0)
    for i in range(GROUP):
        kind, owner = table[KIND + GROUP * step + i], table[OWNER + GROUP * step + i]

        @pl.when(kind == core)
        def _():
            out[i] = mine[owner]

        @pl.when(kind != core)
        def _():
            out[i] = other[owner]


def place(table, mine, other):
    whole = pl.BlockSpec(memory_space=pltpu.VMEM)
    return pl.pallas_call(
        place_body,
        out_shape=jax.ShapeDtypeStruct((BLOCKS, ROWS, WIDTH), bf16),
        grid_spec=pltpu.PrefetchScalarGridSpec(
            num_scalar_prefetch=1,
            grid=(BLOCKS // GROUP,),
            in_specs=[whole, whole],
            out_specs=pl.BlockSpec((GROUP, ROWS, WIDTH), lambda i, table: (i, 0, 0)),
        ),
        compiler_params=params(),
        cost_estimate=cost(0, 4 * BLOCKS * ROWS * WIDTH),
        name="place",
    )(table, mine, other)


def local(grads, assignment, piece_slot, left_roots, right_roots):
    swap = functools.partial(lax.ppermute, axis_name="core", perm=[(0, 1), (1, 0)])
    exchange = functools.partial(lax.all_to_all, axis_name="shard", split_axis=0, concat_axis=0, tiled=True)

    def along(array, shift):
        return lax.ppermute(array, "z", [(z, (z + shift) % DEPTH) for z in range(DEPTH)])

    pieces = grads.reshape(BLOCKS, ROWS, WIDTH)
    table, outgoing = front(assignment, piece_slot, pieces)
    table = pltpu.with_memory_space_constraint(table, pltpu.HBM)
    other = swap(outgoing)

    sums = pair_sum(table, pieces, other)
    parts = [sums[0]] + [along(sums[shift], shift) for shift in ORDER]
    owned = exchange(route(table, other, route(table, pieces)))
    chunk = mean_of(parts)
    chunks = [along(chunk, shift) for shift in reversed(ORDER)] + [chunk]
    owned, *chunks = lax.optimization_barrier((owned, *chunks))
    packed, owned = lax.optimization_barrier((mean_out(table, chunks), owned))
    mean = exchange(packed).reshape(WIDTH, WIDTH)

    terms = gram(owned)
    mean, unused = lax.optimization_barrier((mean, terms))
    share = lax.psum_scatter(terms.reshape(DEPTH * 2 * CHUNK, WIDTH), "z", scatter_dimension=0, tiled=True)
    share = share.reshape(2, CHUNK, WIDTH)
    statistics = statistics_call(table, share, swap(share))

    returned = exchange(precond(table, mean, left_roots, right_roots))
    direction = place(table, returned, swap(returned))
    return statistics, direction.reshape(BLOCKS * ROWS, WIDTH)


def solution(mesh):
    fine = Mesh(mesh.devices.reshape(SHARDS, DEPTH, CORES), ("shard", "z", "core"))
    roots = P("shard", None, None)
    return jax.shard_map(
        local,
        mesh=fine,
        in_specs=(P(("z", "core"), "shard", None), P(), P(), roots, roots),
        out_specs=(P("shard", None, ("z", "core"), None), P("shard", None)),
        check_vma=False,
    )
```

```python
import functools

import jax
import jax.numpy as jnp
from jax import lax
from jax.experimental import pallas as pl
from jax.experimental.pallas import tpu as pltpu
from jax.sharding import Mesh, PartitionSpec as P

epsilon = 1e-06
f32 = jnp.float32
bf16 = jnp.bfloat16

SHARDS, DEPTH, CORES = 16, 8, 2
SLOTS, BLOCKS, ROWS, WIDTH = 2, 18, 64, 1024
HALF = BLOCKS // CORES
CHUNK = WIDTH // DEPTH

ORDER = (4, 3, 5, 2, 6, 1, 7)

OWN, SEND, PLACE, KIND, OWNER, FILLED, SLOTKIND, PICK, USED, SIZE = 0, 9, 18, 34, 52, 70, 72, 74, 75, 128


def params(megabytes=32):
    return pltpu.CompilerParams(vmem_limit_bytes=megabytes * 1024 * 1024)


def cost(flops, moved):
    return pl.CostEstimate(flops=flops, bytes_accessed=moved, transcendentals=0)


def front_body(assignment, piece_slot, pieces, table, out, held, sem):
    shard, core = lax.axis_index("shard"), lax.axis_index("core")
    fetch = pltpu.make_async_copy(pieces, held, sem)
    fetch.start()

    for i in (*range(PLACE, PLACE + SHARDS), *range(FILLED, USED)):
        table[i] = 0
    slots = [assignment[k] for k in range(BLOCKS)]

    def block(k, unused):
        slot, place = assignment[k], piece_slot[k]
        rank = jnp.int32(0)
        for other in slots:
            rank += jnp.where(other < slot, 1, 0)
        kind, index = lax.rem(rank, CORES), lax.div(rank, CORES)
        owner, which = lax.div(slot, SLOTS), lax.rem(slot, SLOTS)
        table[jnp.where(kind == core, OWN, SEND) + index] = place
        table[KIND + place] = kind
        table[OWNER + place] = owner

        @pl.when(kind == core)
        def _():
            table[PLACE + owner] = index

        @pl.when(owner == shard)
        def _():
            table[FILLED + which] = 1
            table[SLOTKIND + which] = kind

        @pl.when((owner == shard) & (kind == core))
        def _():
            table[PICK] = which

        return unused

    lax.fori_loop(0, BLOCKS, block, 0)
    fetch.wait()
    for n in range(HALF):
        out[n] = held[table[SEND + n]]


def front(assignment, piece_slot, pieces):
    smem = pl.BlockSpec(memory_space=pltpu.SMEM)
    return pl.pallas_call(
        front_body,
        out_shape=(
            pltpu.HBM((SIZE,), jnp.int32),
            pltpu.VMEM((HALF, ROWS, WIDTH), bf16),
        ),
        in_specs=[smem, smem, pl.BlockSpec(memory_space=pl.ANY)],
        out_specs=(smem, pl.BlockSpec(memory_space=pltpu.VMEM)),
        scratch_shapes=[pltpu.VMEM((BLOCKS, ROWS, WIDTH), bf16), pltpu.SemaphoreType.DMA],
        compiler_params=params(56),
        cost_estimate=cost(0, 6 * BLOCKS * ROWS * WIDTH),
        name="front",
    )(assignment, piece_slot, pieces)


def pair_sum_body(table, pieces, other, *rest):
    sums, held = rest[:-1], rest[-1]
    me = lax.axis_index("z")

    def add(n, unused):
        held[...] = (pieces[table[OWN + n]].astype(f32) + other[n].astype(f32)).astype(bf16)
        for shift in range(DEPTH):
            target = lax.rem(me + shift, DEPTH)
            sums[shift][n] = held[:, pl.ds(pl.multiple_of(target * CHUNK, CHUNK), CHUNK)]
        return unused

    lax.fori_loop(0, HALF, add, 0)


def pair_sum(table, pieces, other):
    vmem = pl.BlockSpec(memory_space=pltpu.VMEM)
    return pl.pallas_call(
        pair_sum_body,
        out_shape=[jax.ShapeDtypeStruct((HALF, ROWS, CHUNK), bf16)] * DEPTH,
        in_specs=[pl.BlockSpec(memory_space=pltpu.SMEM), vmem, vmem],
        out_specs=[vmem] * DEPTH,
        scratch_shapes=[pltpu.VMEM((ROWS, WIDTH), bf16)],
        compiler_params=params(),
        cost_estimate=cost(HALF * ROWS * WIDTH, 6 * HALF * ROWS * WIDTH),
        name="pair_sum",
    )(table, pieces, other)


TEAM = 4


def route_own_body(table, pieces, routed):
    step = pl.program_id(0)
    for i in range(TEAM):
        routed[i, 0] = pieces[table[OWN + table[PLACE + TEAM * step + i]]]


def route_other_body(table, other, half, routed):
    step = pl.program_id(0)
    for i in range(TEAM):
        routed[i, 0] = other[table[PLACE + TEAM * step + i]]


def route(table, source, half=None):
    part = 0 if half is None else 1
    block = pl.BlockSpec((TEAM, 1, ROWS, WIDTH), lambda i, table: (i, part, 0, 0))
    return pl.pallas_call(
        route_other_body if part else route_own_body,
        out_shape=pltpu.HBM((SHARDS, CORES, ROWS, WIDTH), bf16),
        grid_spec=pltpu.PrefetchScalarGridSpec(
            num_scalar_prefetch=1,
            grid=(SHARDS // TEAM,),
            in_specs=[pl.BlockSpec(memory_space=pltpu.VMEM)] + [pl.BlockSpec(memory_space=pl.ANY)] * part,
            out_specs=block,
        ),
        input_output_aliases={2: 0} if part else {},
        compiler_params=params(),
        cost_estimate=cost(0, 4 * SHARDS * ROWS * WIDTH),
        name="route_other" if part else "route_own",
    )(table, source, *([half] if part else []))


def mean_body(*refs):
    parts, out = refs[:-1], refs[-1]
    for n in range(HALF):
        total = parts[0][n].astype(f32)
        for part in parts[1:]:
            total += part[n].astype(f32)
        out[n] = (total * (1.0 / (DEPTH * CORES))).astype(bf16)


def mean_of(parts):
    vmem = pl.BlockSpec(memory_space=pltpu.VMEM)
    return pl.pallas_call(
        mean_body,
        out_shape=jax.ShapeDtypeStruct((HALF, ROWS, CHUNK), bf16),
        in_specs=[vmem] * DEPTH,
        out_specs=vmem,
        compiler_params=params(),
        cost_estimate=cost(DEPTH * HALF * ROWS * CHUNK, 18 * HALF * ROWS * CHUNK),
        name="mean",
    )(*parts)


def mean_out_body(table, *refs):
    chunks, out = refs[:-1], refs[-1]
    me, step = lax.axis_index("z"), pl.program_id(0)

    def one(i, unused):
        index = table[PLACE + TEAM * step + i]
        for shift, chunk in enumerate(chunks):
            source = lax.rem(me + DEPTH - shift, DEPTH)
            columns = pl.ds(pl.multiple_of(source * CHUNK, CHUNK), CHUNK)
            out[i, :, columns] = chunk[index]
        return unused

    lax.fori_loop(0, TEAM, one, 0)


def mean_out(table, chunks):
    return pl.pallas_call(
        mean_out_body,
        out_shape=pltpu.HBM((SHARDS, ROWS, WIDTH), bf16),
        grid_spec=pltpu.PrefetchScalarGridSpec(
            num_scalar_prefetch=1,
            grid=(SHARDS // TEAM,),
            in_specs=[pl.BlockSpec(memory_space=pltpu.VMEM)] * DEPTH,
            out_specs=pl.BlockSpec((TEAM, ROWS, WIDTH), lambda i, table: (i, 0, 0)),
        ),
        compiler_params=params(),
        cost_estimate=cost(0, 4 * SHARDS * ROWS * WIDTH),
        name="mean_out",
    )(table, *chunks)


STEPS = 4
STRIP = WIDTH // STEPS
LONG = WIDTH // 2


def precond_body(table, mean, left, right, out, roots, middle, scaled, sums, sems):
    slot = table[PICK]
    second = pltpu.make_async_copy(right.at[slot], roots.at[1], sems.at[STEPS])
    first = pltpu.make_async_copy(left.at[slot], roots.at[0], sems.at[STEPS + 1])
    second.start()
    first.start()
    sums[...] = jnp.zeros_like(sums)
    group = LONG // ROWS

    def power(step, unused):
        own = mean[pl.ds(pl.multiple_of(step * STRIP, STRIP), STRIP), :].astype(f32)
        sums[0:1, :] += jnp.sum(own * own, axis=0, keepdims=True)
        return unused

    lax.fori_loop(0, STEPS, power, 0)
    second.wait()

    def apply_right(step, unused):
        rows = pl.ds(pl.multiple_of(step * LONG, LONG), LONG)
        middle[rows, :] = jnp.dot(mean[rows, :], roots[1], preferred_element_type=f32).astype(bf16)
        return unused

    lax.fori_loop(0, WIDTH // LONG, apply_right, 0)
    first.wait()

    def apply_left(step, unused):
        rows = pl.ds(pl.multiple_of(step * LONG, LONG), LONG)
        product = jnp.dot(roots[0, rows, :], middle[...], preferred_element_type=f32).astype(bf16)
        wide = product.astype(f32)
        sums[1:2, :] += jnp.sum(wide * wide, axis=0, keepdims=True)
        scaled[pl.ds(step * group, group)] = product.reshape(group, ROWS, WIDTH)
        return unused

    lax.fori_loop(0, WIDTH // LONG, apply_left, 0)
    grad_power = jnp.sum(sums[0:1, :], axis=1, keepdims=True) * (1.0 / (WIDTH * WIDTH))
    pre_power = jnp.sum(sums[1:2, :], axis=1, keepdims=True) * (1.0 / (WIDTH * WIDTH))
    factor = jnp.sqrt((grad_power + epsilon) / (pre_power + epsilon))
    sends = []
    for step in range(STEPS):
        part = pl.ds(step * TEAM, TEAM)

        def scale(i, unused, step=step):
            scaled[step * TEAM + i] = (scaled[step * TEAM + i].astype(f32) * factor).astype(bf16)
            return unused

        lax.fori_loop(0, TEAM, scale, 0)
        sends.append(pltpu.make_async_copy(scaled.at[part], out.at[part], sems.at[step]))
        sends[-1].start()
    for send in sends:
        send.wait()


def precond(table, mean, left_roots, right_roots):
    anywhere = pl.BlockSpec(memory_space=pl.ANY)
    left_roots = pltpu.with_memory_space_constraint(left_roots, pltpu.HBM)
    right_roots = pltpu.with_memory_space_constraint(right_roots, pltpu.HBM)
    return pl.pallas_call(
        precond_body,
        out_shape=pltpu.HBM((SHARDS, ROWS, WIDTH), bf16),
        in_specs=[
            pl.BlockSpec(memory_space=pltpu.SMEM),
            pl.BlockSpec(memory_space=pltpu.VMEM),
            anywhere,
            anywhere,
        ],
        out_specs=anywhere,
        scratch_shapes=[
            pltpu.VMEM((2, WIDTH, WIDTH), bf16),
            pltpu.VMEM((WIDTH, WIDTH), bf16),
            pltpu.VMEM((SHARDS, ROWS, WIDTH), bf16),
            pltpu.VMEM((8, WIDTH), f32),
            pltpu.SemaphoreType.DMA((STEPS + 2,)),
        ],
        compiler_params=params(),
        cost_estimate=cost(80 * WIDTH**3, 8 * WIDTH**2),
        name="precond",
    )(table, mean, left_roots, right_roots)


def gram_body(grads, out, whole, terms, sems):
    scale = 1.0 / (WIDTH * DEPTH * CORES)
    per = STRIP // CHUNK
    for rep in range(CORES):
        whole[rep] = grads[:, rep].reshape(WIDTH, WIDTH)
    sends = []
    for step in range(STEPS):
        here = slice(step * STRIP, (step + 1) * STRIP)
        rest = slice(step * STRIP, WIDTH)
        left = right = None
        for rep in range(CORES):
            first = lax.dot_general(
                whole[rep, here, :], whole[rep, rest, :], (((1,), (1,)), ((), ())), preferred_element_type=f32
            )
            second = lax.dot_general(
                whole[rep, :, here], whole[rep, :, rest], (((0,), (0,)), ((), ())), preferred_element_type=f32
            )
            left = first if left is None else left + first
            right = second if right is None else right + second
        for side, value in enumerate((left, right)):
            value = value * scale
            terms[step * per : (step + 1) * per, side, :, rest] = value.astype(bf16).reshape(per, CHUNK, -1)
            for other in range(step + 1, STEPS):
                offset = (other - step) * STRIP
                cell = value[:, offset : offset + STRIP].T.astype(bf16).reshape(per, CHUNK, STRIP)
                terms[other * per : (other + 1) * per, side, :, here] = cell
        part = pl.ds(step * per, per)
        sends.append(pltpu.make_async_copy(terms.at[part], out.at[part], sems.at[step]))
        sends[-1].start()
    for send in sends:
        send.wait()


def gram(grads):
    return pl.pallas_call(
        gram_body,
        out_shape=pltpu.HBM((DEPTH, 2, CHUNK, WIDTH), bf16),
        in_specs=[pl.BlockSpec(memory_space=pltpu.VMEM)],
        out_specs=pl.BlockSpec(memory_space=pl.ANY),
        scratch_shapes=[
            pltpu.VMEM((CORES, WIDTH, WIDTH), bf16),
            pltpu.VMEM((DEPTH, 2, CHUNK, WIDTH), bf16),
            pltpu.SemaphoreType.DMA((STEPS,)),
        ],
        compiler_params=params(),
        cost_estimate=cost(8 * WIDTH**3, 8 * WIDTH**2),
        name="gram",
    )(grads)


GROUP = 6


def finish_body(table, returned, swapped, share, other, direction, statistics):
    core = lax.axis_index("core")
    step = pl.program_id(0)
    for i in range(GROUP):
        kind, owner = table[KIND + GROUP * step + i], table[OWNER + GROUP * step + i]

        @pl.when(kind == core)
        def _():
            direction[i] = returned[owner]

        @pl.when(kind != core)
        def _():
            direction[i] = swapped[owner]

    @pl.when(step == 0)
    def _():
        rows = pl.ds(pl.multiple_of(core * ROWS, ROWS), ROWS)
        for slot in range(SLOTS):
            for side in range(2):
                kept = share[side, rows, :].astype(f32)
                got = other[side, rows, :].astype(f32)
                value = jnp.where(table[SLOTKIND + slot] == core, kept, got)
                statistics[slot, side] = jnp.where(table[FILLED + slot] == 1, value, 0.0)


def finish(table, returned, swapped, share, other):
    return pl.pallas_call(
        finish_body,
        out_shape=(
            jax.ShapeDtypeStruct((BLOCKS, ROWS, WIDTH), bf16),
            jax.ShapeDtypeStruct((SLOTS, 2, ROWS, WIDTH), f32),
        ),
        grid_spec=pltpu.PrefetchScalarGridSpec(
            num_scalar_prefetch=1,
            grid=(BLOCKS // GROUP,),
            in_specs=[pl.BlockSpec(memory_space=pltpu.VMEM)] * 4,
            out_specs=(
                pl.BlockSpec((GROUP, ROWS, WIDTH), lambda i, table: (i, 0, 0)),
                pl.BlockSpec((SLOTS, 2, ROWS, WIDTH), lambda i, table: (0, 0, 0, 0)),
            ),
        ),
        compiler_params=params(),
        cost_estimate=cost(0, 24 * BLOCKS * ROWS * WIDTH),
        name="finish",
    )(table, returned, swapped, share, other)


def local(grads, assignment, piece_slot, left_roots, right_roots):
    swap = functools.partial(lax.ppermute, axis_name="core", perm=[(0, 1), (1, 0)])
    exchange = functools.partial(lax.all_to_all, axis_name="shard", split_axis=0, concat_axis=0, tiled=True)

    def along(array, shift):
        return lax.ppermute(array, "z", [(z, (z + shift) % DEPTH) for z in range(DEPTH)])

    pieces = grads.reshape(BLOCKS, ROWS, WIDTH)
    table, outgoing = front(assignment, piece_slot, pieces)
    table = pltpu.with_memory_space_constraint(table, pltpu.HBM)
    other = swap(outgoing)

    sums = pair_sum(table, pieces, other)
    parts = [sums[0]] + [along(sums[shift], shift) for shift in ORDER]
    owned = exchange(route(table, other, route(table, pieces)))
    chunk = mean_of(parts)
    chunks = {0: chunk} | {shift: along(chunk, shift) for shift in (2, 6, 1, 7)}
    chunks |= {4: along(chunks[2], 2), 3: along(chunks[2], 1), 5: along(chunks[6], 7)}
    chunks = [chunks[shift] for shift in range(DEPTH)]
    owned, *chunks = lax.optimization_barrier((owned, *chunks))
    packed, owned = lax.optimization_barrier((mean_out(table, chunks), owned))
    mean = exchange(packed).reshape(WIDTH, WIDTH)

    terms = gram(owned)
    mean, unused = lax.optimization_barrier((mean, terms))
    share = lax.psum_scatter(terms.reshape(DEPTH * 2 * CHUNK, WIDTH), "z", scatter_dimension=0, tiled=True)
    share = share.reshape(2, CHUNK, WIDTH)

    returned = exchange(precond(table, mean, left_roots, right_roots))
    direction, statistics = finish(table, returned, swap(returned), share, swap(share))
    return statistics, direction.reshape(BLOCKS * ROWS, WIDTH)


def solution(mesh):
    fine = Mesh(mesh.devices.reshape(SHARDS, DEPTH, CORES), ("shard", "z", "core"))
    roots = P("shard", None, None)
    return jax.shard_map(
        local,
        mesh=fine,
        in_specs=(P(("z", "core"), "shard", None), P(), P(), roots, roots),
        out_specs=(P("shard", None, ("z", "core"), None), P("shard", None)),
        check_vma=False,
    )
```

```python
import functools

import jax
import jax.numpy as jnp
from jax import lax
from jax.experimental import pallas as pl
from jax.experimental.pallas import tpu as pltpu
from jax.sharding import Mesh, PartitionSpec as P

epsilon = 1e-06
f32 = jnp.float32
bf16 = jnp.bfloat16

SHARDS, DEPTH, CORES = 16, 8, 2
SLOTS, BLOCKS, ROWS, WIDTH = 2, 18, 64, 1024
HALF = BLOCKS // CORES
CHUNK = WIDTH // DEPTH

ORDER = (4, 3, 5, 2, 6, 1, 7)
HOPS = (2, 6, 1, 7, 4, 3, 5, 0)

OWN, SEND, PLACE, KIND, OWNER, FILLED, SLOTKIND, PICK, USED, SIZE = 0, 9, 18, 34, 52, 70, 72, 74, 75, 128


def params(megabytes=32):
    return pltpu.CompilerParams(vmem_limit_bytes=megabytes * 1024 * 1024)


def cost(flops, moved):
    return pl.CostEstimate(flops=flops, bytes_accessed=moved, transcendentals=0)


def front_body(assignment, piece_slot, pieces, table, out, held, sem):
    shard, core = lax.axis_index("shard"), lax.axis_index("core")
    fetch = pltpu.make_async_copy(pieces, held, sem)
    fetch.start()

    for i in (*range(PLACE, PLACE + SHARDS), *range(FILLED, USED)):
        table[i] = 0
    slots = [assignment[k] for k in range(BLOCKS)]

    def block(k, unused):
        slot, place = assignment[k], piece_slot[k]
        rank = jnp.int32(0)
        for other in slots:
            rank += jnp.where(other < slot, 1, 0)
        kind, index = lax.rem(rank, CORES), lax.div(rank, CORES)
        owner, which = lax.div(slot, SLOTS), lax.rem(slot, SLOTS)
        table[jnp.where(kind == core, OWN, SEND) + index] = place
        table[KIND + place] = kind
        table[OWNER + place] = owner

        @pl.when(kind == core)
        def _():
            table[PLACE + owner] = index

        @pl.when(owner == shard)
        def _():
            table[FILLED + which] = 1
            table[SLOTKIND + which] = kind

        @pl.when((owner == shard) & (kind == core))
        def _():
            table[PICK] = which

        return unused

    lax.fori_loop(0, BLOCKS, block, 0)
    fetch.wait()
    for n in range(HALF):
        out[n] = held[table[SEND + n]]


def front(assignment, piece_slot, pieces):
    smem = pl.BlockSpec(memory_space=pltpu.SMEM)
    return pl.pallas_call(
        front_body,
        out_shape=(
            pltpu.HBM((SIZE,), jnp.int32),
            pltpu.VMEM((HALF, ROWS, WIDTH), bf16),
        ),
        in_specs=[smem, smem, pl.BlockSpec(memory_space=pl.ANY)],
        out_specs=(smem, pl.BlockSpec(memory_space=pltpu.VMEM)),
        scratch_shapes=[pltpu.VMEM((BLOCKS, ROWS, WIDTH), bf16), pltpu.SemaphoreType.DMA],
        compiler_params=params(56),
        cost_estimate=cost(0, 6 * BLOCKS * ROWS * WIDTH),
        name="front",
    )(assignment, piece_slot, pieces)


def pair_sum_body(table, pieces, other, *rest):
    sums, held = rest[:-1], rest[-1]
    me = lax.axis_index("z")

    def add(n, unused):
        held[...] = (pieces[table[OWN + n]].astype(f32) + other[n].astype(f32)).astype(bf16)
        for shift in range(DEPTH):
            target = lax.rem(me + shift, DEPTH)
            sums[shift][n] = held[:, pl.ds(pl.multiple_of(target * CHUNK, CHUNK), CHUNK)]
        return unused

    lax.fori_loop(0, HALF, add, 0)


def pair_sum(table, pieces, other):
    vmem = pl.BlockSpec(memory_space=pltpu.VMEM)
    return pl.pallas_call(
        pair_sum_body,
        out_shape=[jax.ShapeDtypeStruct((HALF, ROWS, CHUNK), bf16)] * DEPTH,
        in_specs=[pl.BlockSpec(memory_space=pltpu.SMEM), vmem, vmem],
        out_specs=[vmem] * DEPTH,
        scratch_shapes=[pltpu.VMEM((ROWS, WIDTH), bf16)],
        compiler_params=params(),
        cost_estimate=cost(HALF * ROWS * WIDTH, 6 * HALF * ROWS * WIDTH),
        name="pair_sum",
    )(table, pieces, other)


TEAM = 4


def route_own_body(table, pieces, routed):
    step = pl.program_id(0)
    for i in range(TEAM):
        routed[i, 0] = pieces[table[OWN + table[PLACE + TEAM * step + i]]]


def route_other_body(table, other, half, routed):
    step = pl.program_id(0)
    for i in range(TEAM):
        routed[i, 0] = other[table[PLACE + TEAM * step + i]]


def route(table, source, half=None):
    part = 0 if half is None else 1
    block = pl.BlockSpec((TEAM, 1, ROWS, WIDTH), lambda i, table: (i, part, 0, 0))
    return pl.pallas_call(
        route_other_body if part else route_own_body,
        out_shape=pltpu.HBM((SHARDS, CORES, ROWS, WIDTH), bf16),
        grid_spec=pltpu.PrefetchScalarGridSpec(
            num_scalar_prefetch=1,
            grid=(SHARDS // TEAM,),
            in_specs=[pl.BlockSpec(memory_space=pltpu.VMEM)] + [pl.BlockSpec(memory_space=pl.ANY)] * part,
            out_specs=block,
        ),
        input_output_aliases={2: 0} if part else {},
        compiler_params=params(),
        cost_estimate=cost(0, 4 * SHARDS * ROWS * WIDTH),
        name="route_other" if part else "route_own",
    )(table, source, *([half] if part else []))


def mean_body(*refs):
    parts, out = refs[:-1], refs[-1]
    for n in range(HALF):
        total = parts[0][n].astype(f32)
        for part in parts[1:]:
            total += part[n].astype(f32)
        out[n] = (total * (1.0 / (DEPTH * CORES))).astype(bf16)


def mean_of(parts):
    vmem = pl.BlockSpec(memory_space=pltpu.VMEM)
    return pl.pallas_call(
        mean_body,
        out_shape=jax.ShapeDtypeStruct((HALF, ROWS, CHUNK), bf16),
        in_specs=[vmem] * DEPTH,
        out_specs=vmem,
        compiler_params=params(),
        cost_estimate=cost(DEPTH * HALF * ROWS * CHUNK, 18 * HALF * ROWS * CHUNK),
        name="mean",
    )(*parts)


def mean_out_body(table, *refs):
    chunks, out = refs[:-1], refs[-1]
    me, step = lax.axis_index("z"), pl.program_id(0)

    def one(i, unused):
        index = table[PLACE + TEAM * step + i]
        for shift, chunk in zip(HOPS, chunks):
            source = lax.rem(me + DEPTH - shift, DEPTH)
            columns = pl.ds(pl.multiple_of(source * CHUNK, CHUNK), CHUNK)
            out[i, :, columns] = chunk[index]
        return unused

    lax.fori_loop(0, TEAM, one, 0)


def mean_out(table, chunks):
    return pl.pallas_call(
        mean_out_body,
        out_shape=pltpu.HBM((SHARDS, ROWS, WIDTH), bf16),
        grid_spec=pltpu.PrefetchScalarGridSpec(
            num_scalar_prefetch=1,
            grid=(SHARDS // TEAM,),
            in_specs=[pl.BlockSpec(memory_space=pltpu.VMEM)] * DEPTH,
            out_specs=pl.BlockSpec((TEAM, ROWS, WIDTH), lambda i, table: (i, 0, 0)),
        ),
        compiler_params=params(),
        cost_estimate=cost(0, 4 * SHARDS * ROWS * WIDTH),
        name="mean_out",
    )(table, *chunks)


STEPS = 4
STRIP = WIDTH // STEPS
LONG = WIDTH // 2


def precond_body(table, mean, left, right, out, roots, middle, scaled, sums, sems):
    slot = table[PICK]
    second = pltpu.make_async_copy(right.at[slot], roots.at[1], sems.at[STEPS])
    first = pltpu.make_async_copy(left.at[slot], roots.at[0], sems.at[STEPS + 1])
    second.start()
    first.start()
    sums[...] = jnp.zeros_like(sums)
    group = LONG // ROWS

    def power(step, unused):
        own = mean[pl.ds(pl.multiple_of(step * STRIP, STRIP), STRIP), :].astype(f32)
        sums[0:1, :] += jnp.sum(own * own, axis=0, keepdims=True)
        return unused

    lax.fori_loop(0, STEPS, power, 0)
    second.wait()

    def apply_right(step, unused):
        rows = pl.ds(pl.multiple_of(step * LONG, LONG), LONG)
        middle[rows, :] = jnp.dot(mean[rows, :], roots[1], preferred_element_type=f32).astype(bf16)
        return unused

    lax.fori_loop(0, WIDTH // LONG, apply_right, 0)
    first.wait()

    def apply_left(step, unused):
        rows = pl.ds(pl.multiple_of(step * LONG, LONG), LONG)
        product = jnp.dot(roots[0, rows, :], middle[...], preferred_element_type=f32).astype(bf16)
        wide = product.astype(f32)
        sums[1:2, :] += jnp.sum(wide * wide, axis=0, keepdims=True)
        scaled[pl.ds(step * group, group)] = product.reshape(group, ROWS, WIDTH)
        return unused

    lax.fori_loop(0, WIDTH // LONG, apply_left, 0)
    grad_power = jnp.sum(sums[0:1, :], axis=1, keepdims=True) * (1.0 / (WIDTH * WIDTH))
    pre_power = jnp.sum(sums[1:2, :], axis=1, keepdims=True) * (1.0 / (WIDTH * WIDTH))
    factor = jnp.sqrt((grad_power + epsilon) / (pre_power + epsilon))
    sends = []
    for step in range(STEPS):
        part = pl.ds(step * TEAM, TEAM)

        def scale(i, unused, step=step):
            scaled[step * TEAM + i] = (scaled[step * TEAM + i].astype(f32) * factor).astype(bf16)
            return unused

        lax.fori_loop(0, TEAM, scale, 0)
        sends.append(pltpu.make_async_copy(scaled.at[part], out.at[part], sems.at[step]))
        sends[-1].start()
    for send in sends:
        send.wait()


def precond(table, mean, left_roots, right_roots):
    anywhere = pl.BlockSpec(memory_space=pl.ANY)
    left_roots = pltpu.with_memory_space_constraint(left_roots, pltpu.HBM)
    right_roots = pltpu.with_memory_space_constraint(right_roots, pltpu.HBM)
    return pl.pallas_call(
        precond_body,
        out_shape=pltpu.HBM((SHARDS, ROWS, WIDTH), bf16),
        in_specs=[
            pl.BlockSpec(memory_space=pltpu.SMEM),
            pl.BlockSpec(memory_space=pltpu.VMEM),
            anywhere,
            anywhere,
        ],
        out_specs=anywhere,
        scratch_shapes=[
            pltpu.VMEM((2, WIDTH, WIDTH), bf16),
            pltpu.VMEM((WIDTH, WIDTH), bf16),
            pltpu.VMEM((SHARDS, ROWS, WIDTH), bf16),
            pltpu.VMEM((8, WIDTH), f32),
            pltpu.SemaphoreType.DMA((STEPS + 2,)),
        ],
        compiler_params=params(),
        cost_estimate=cost(80 * WIDTH**3, 8 * WIDTH**2),
        name="precond",
    )(table, mean, left_roots, right_roots)


def gram_body(grads, out, whole, terms, sems):
    scale = 1.0 / (WIDTH * DEPTH * CORES)
    per = STRIP // CHUNK
    for rep in range(CORES):
        whole[rep] = grads[:, rep].reshape(WIDTH, WIDTH)
    sends = []
    for step in range(STEPS):
        here = slice(step * STRIP, (step + 1) * STRIP)
        rest = slice(step * STRIP, WIDTH)
        left = right = None
        for rep in range(CORES):
            first = lax.dot_general(
                whole[rep, here, :], whole[rep, rest, :], (((1,), (1,)), ((), ())), preferred_element_type=f32
            )
            second = lax.dot_general(
                whole[rep, :, here], whole[rep, :, rest], (((0,), (0,)), ((), ())), preferred_element_type=f32
            )
            left = first if left is None else left + first
            right = second if right is None else right + second
        for side, value in enumerate((left, right)):
            value = value * scale
            terms[step * per : (step + 1) * per, side, :, rest] = value.astype(bf16).reshape(per, CHUNK, -1)
            for other in range(step + 1, STEPS):
                offset = (other - step) * STRIP
                cell = value[:, offset : offset + STRIP].T.astype(bf16).reshape(per, CHUNK, STRIP)
                terms[other * per : (other + 1) * per, side, :, here] = cell
        part = pl.ds(step * per, per)
        sends.append(pltpu.make_async_copy(terms.at[part], out.at[part], sems.at[step]))
        sends[-1].start()
    for send in sends:
        send.wait()


def gram(grads):
    return pl.pallas_call(
        gram_body,
        out_shape=pltpu.HBM((DEPTH, 2, CHUNK, WIDTH), bf16),
        in_specs=[pl.BlockSpec(memory_space=pltpu.VMEM)],
        out_specs=pl.BlockSpec(memory_space=pl.ANY),
        scratch_shapes=[
            pltpu.VMEM((CORES, WIDTH, WIDTH), bf16),
            pltpu.VMEM((DEPTH, 2, CHUNK, WIDTH), bf16),
            pltpu.SemaphoreType.DMA((STEPS,)),
        ],
        compiler_params=params(),
        cost_estimate=cost(8 * WIDTH**3, 8 * WIDTH**2),
        name="gram",
    )(grads)


GROUP = 6


def finish_body(table, returned, swapped, share, other, direction, statistics):
    core = lax.axis_index("core")
    step = pl.program_id(0)
    for i in range(GROUP):
        kind, owner = table[KIND + GROUP * step + i], table[OWNER + GROUP * step + i]

        @pl.when(kind == core)
        def _():
            direction[i] = returned[owner]

        @pl.when(kind != core)
        def _():
            direction[i] = swapped[owner]

    @pl.when(step == 0)
    def _():
        rows = pl.ds(pl.multiple_of(core * ROWS, ROWS), ROWS)
        for slot in range(SLOTS):
            for side in range(2):
                kept = share[side, rows, :].astype(f32)
                got = other[side, rows, :].astype(f32)
                value = jnp.where(table[SLOTKIND + slot] == core, kept, got)
                statistics[slot, side] = jnp.where(table[FILLED + slot] == 1, value, 0.0)


def finish(table, returned, swapped, share, other):
    return pl.pallas_call(
        finish_body,
        out_shape=(
            jax.ShapeDtypeStruct((BLOCKS, ROWS, WIDTH), bf16),
            jax.ShapeDtypeStruct((SLOTS, 2, ROWS, WIDTH), f32),
        ),
        grid_spec=pltpu.PrefetchScalarGridSpec(
            num_scalar_prefetch=1,
            grid=(BLOCKS // GROUP,),
            in_specs=[pl.BlockSpec(memory_space=pltpu.VMEM)] * 4,
            out_specs=(
                pl.BlockSpec((GROUP, ROWS, WIDTH), lambda i, table: (i, 0, 0)),
                pl.BlockSpec((SLOTS, 2, ROWS, WIDTH), lambda i, table: (0, 0, 0, 0)),
            ),
        ),
        compiler_params=params(),
        cost_estimate=cost(0, 24 * BLOCKS * ROWS * WIDTH),
        name="finish",
    )(table, returned, swapped, share, other)


def local(grads, assignment, piece_slot, left_roots, right_roots):
    swap = functools.partial(lax.ppermute, axis_name="core", perm=[(0, 1), (1, 0)])
    exchange = functools.partial(lax.all_to_all, axis_name="shard", split_axis=0, concat_axis=0, tiled=True)

    def along(array, shift):
        return lax.ppermute(array, "z", [(z, (z + shift) % DEPTH) for z in range(DEPTH)])

    pieces = grads.reshape(BLOCKS, ROWS, WIDTH)
    table, outgoing = front(assignment, piece_slot, pieces)
    table = pltpu.with_memory_space_constraint(table, pltpu.HBM)
    other = swap(outgoing)

    sums = pair_sum(table, pieces, other)
    parts = [sums[0]] + [along(sums[shift], shift) for shift in ORDER]
    owned = exchange(route(table, other, route(table, pieces)))
    chunk = mean_of(parts)
    chunks = {0: chunk} | {shift: along(chunk, shift) for shift in (2, 6, 1, 7)}
    chunks |= {4: along(chunks[2], 2), 3: along(chunks[2], 1), 5: along(chunks[6], 7)}
    chunks = [chunks[shift] for shift in HOPS]
    packed, owned = lax.optimization_barrier((mean_out(table, chunks), owned))
    mean = exchange(packed).reshape(WIDTH, WIDTH)

    terms = gram(owned)
    mean, unused = lax.optimization_barrier((mean, terms))
    share = lax.psum_scatter(terms.reshape(DEPTH * 2 * CHUNK, WIDTH), "z", scatter_dimension=0, tiled=True)
    share = share.reshape(2, CHUNK, WIDTH)

    returned = exchange(precond(table, mean, left_roots, right_roots))
    direction, statistics = finish(table, returned, swap(returned), share, swap(share))
    return statistics, direction.reshape(BLOCKS * ROWS, WIDTH)


def solution(mesh):
    fine = Mesh(mesh.devices.reshape(SHARDS, DEPTH, CORES), ("shard", "z", "core"))
    roots = P("shard", None, None)
    return jax.shard_map(
        local,
        mesh=fine,
        in_specs=(P(("z", "core"), "shard", None), P(), P(), roots, roots),
        out_specs=(P("shard", None, ("z", "core"), None), P("shard", None)),
        check_vma=False,
    )
```

```python
import functools

import jax
import jax.numpy as jnp
from jax import lax
from jax.experimental import pallas as pl
from jax.experimental.pallas import tpu as pltpu
from jax.sharding import Mesh, PartitionSpec as P

epsilon = 1e-06
f32 = jnp.float32
bf16 = jnp.bfloat16

SHARDS, DEPTH, CORES = 16, 8, 2
SLOTS, BLOCKS, ROWS, WIDTH = 2, 18, 64, 1024
HALF = BLOCKS // CORES
CHUNK = WIDTH // DEPTH

ORDER = (3, 5, 4, 2, 6, 1, 7)
HOPS = (2, 6, 1, 7, 4, 3, 5, 0)

OWN, SEND, PLACE, KIND, OWNER, FILLED, SLOTKIND, PICK, USED, SIZE = 0, 9, 18, 34, 52, 70, 72, 74, 75, 128


def params(megabytes=32):
    return pltpu.CompilerParams(vmem_limit_bytes=megabytes * 1024 * 1024)


def cost(flops, moved):
    return pl.CostEstimate(flops=flops, bytes_accessed=moved, transcendentals=0)


def front_body(assignment, piece_slot, pieces, table, out, held, sem):
    shard, core = lax.axis_index("shard"), lax.axis_index("core")
    fetch = pltpu.make_async_copy(pieces, held, sem)
    fetch.start()

    for i in (*range(PLACE, PLACE + SHARDS), *range(FILLED, USED)):
        table[i] = 0
    slots = [assignment[k] for k in range(BLOCKS)]

    def block(k, unused):
        slot, place = assignment[k], piece_slot[k]
        rank = jnp.int32(0)
        for other in slots:
            rank += jnp.where(other < slot, 1, 0)
        kind, index = lax.rem(rank, CORES), lax.div(rank, CORES)
        owner, which = lax.div(slot, SLOTS), lax.rem(slot, SLOTS)
        table[jnp.where(kind == core, OWN, SEND) + index] = place
        table[KIND + place] = kind
        table[OWNER + place] = owner

        @pl.when(kind == core)
        def _():
            table[PLACE + owner] = index

        @pl.when(owner == shard)
        def _():
            table[FILLED + which] = 1
            table[SLOTKIND + which] = kind

        @pl.when((owner == shard) & (kind == core))
        def _():
            table[PICK] = which

        return unused

    lax.fori_loop(0, BLOCKS, block, 0)
    fetch.wait()
    for n in range(HALF):
        out[n] = held[table[SEND + n]]


def front(assignment, piece_slot, pieces):
    smem = pl.BlockSpec(memory_space=pltpu.SMEM)
    return pl.pallas_call(
        front_body,
        out_shape=(
            pltpu.HBM((SIZE,), jnp.int32),
            pltpu.VMEM((HALF, ROWS, WIDTH), bf16),
        ),
        in_specs=[smem, smem, pl.BlockSpec(memory_space=pl.ANY)],
        out_specs=(smem, pl.BlockSpec(memory_space=pltpu.VMEM)),
        scratch_shapes=[pltpu.VMEM((BLOCKS, ROWS, WIDTH), bf16), pltpu.SemaphoreType.DMA],
        compiler_params=params(56),
        cost_estimate=cost(0, 6 * BLOCKS * ROWS * WIDTH),
        name="front",
    )(assignment, piece_slot, pieces)


def pair_sum_body(table, pieces, other, *rest):
    sums, held = rest[:-1], rest[-1]
    me = lax.axis_index("z")

    def add(n, unused):
        held[...] = (pieces[table[OWN + n]].astype(f32) + other[n].astype(f32)).astype(bf16)
        for shift in range(DEPTH):
            target = lax.rem(me + shift, DEPTH)
            sums[shift][n] = held[:, pl.ds(pl.multiple_of(target * CHUNK, CHUNK), CHUNK)]
        return unused

    lax.fori_loop(0, HALF, add, 0)


def pair_sum(table, pieces, other):
    vmem = pl.BlockSpec(memory_space=pltpu.VMEM)
    return pl.pallas_call(
        pair_sum_body,
        out_shape=[jax.ShapeDtypeStruct((HALF, ROWS, CHUNK), bf16)] * DEPTH,
        in_specs=[pl.BlockSpec(memory_space=pltpu.SMEM), vmem, vmem],
        out_specs=[vmem] * DEPTH,
        scratch_shapes=[pltpu.VMEM((ROWS, WIDTH), bf16)],
        compiler_params=params(),
        cost_estimate=cost(HALF * ROWS * WIDTH, 6 * HALF * ROWS * WIDTH),
        name="pair_sum",
    )(table, pieces, other)


TEAM = 4


def route_own_body(table, pieces, routed):
    step = pl.program_id(0)
    for i in range(TEAM):
        routed[i, 0] = pieces[table[OWN + table[PLACE + TEAM * step + i]]]


def route_other_body(table, other, half, routed):
    step = pl.program_id(0)
    for i in range(TEAM):
        routed[i, 0] = other[table[PLACE + TEAM * step + i]]


def route(table, source, half=None):
    part = 0 if half is None else 1
    block = pl.BlockSpec((TEAM, 1, ROWS, WIDTH), lambda i, table: (i, part, 0, 0))
    return pl.pallas_call(
        route_other_body if part else route_own_body,
        out_shape=pltpu.HBM((SHARDS, CORES, ROWS, WIDTH), bf16),
        grid_spec=pltpu.PrefetchScalarGridSpec(
            num_scalar_prefetch=1,
            grid=(SHARDS // TEAM,),
            in_specs=[pl.BlockSpec(memory_space=pltpu.VMEM)] + [pl.BlockSpec(memory_space=pl.ANY)] * part,
            out_specs=block,
        ),
        input_output_aliases={2: 0} if part else {},
        compiler_params=params(),
        cost_estimate=cost(0, 4 * SHARDS * ROWS * WIDTH),
        name="route_other" if part else "route_own",
    )(table, source, *([half] if part else []))


def mean_body(*refs):
    parts, out = refs[:-1], refs[-1]
    for n in range(HALF):
        total = parts[0][n].astype(f32)
        for part in parts[1:]:
            total += part[n].astype(f32)
        out[n] = (total * (1.0 / (DEPTH * CORES))).astype(bf16)


def mean_of(parts):
    vmem = pl.BlockSpec(memory_space=pltpu.VMEM)
    return pl.pallas_call(
        mean_body,
        out_shape=jax.ShapeDtypeStruct((HALF, ROWS, CHUNK), bf16),
        in_specs=[vmem] * DEPTH,
        out_specs=vmem,
        compiler_params=params(),
        cost_estimate=cost(DEPTH * HALF * ROWS * CHUNK, 18 * HALF * ROWS * CHUNK),
        name="mean",
    )(*parts)


def mean_out_body(table, *refs):
    chunks, out = refs[:-1], refs[-1]
    me, step = lax.axis_index("z"), pl.program_id(0)

    def one(i, unused):
        index = table[PLACE + TEAM * step + i]
        for shift, chunk in zip(HOPS, chunks):
            source = lax.rem(me + DEPTH - shift, DEPTH)
            columns = pl.ds(pl.multiple_of(source * CHUNK, CHUNK), CHUNK)
            out[i, :, columns] = chunk[index]
        return unused

    lax.fori_loop(0, TEAM, one, 0)


def mean_out(table, chunks):
    return pl.pallas_call(
        mean_out_body,
        out_shape=pltpu.HBM((SHARDS, ROWS, WIDTH), bf16),
        grid_spec=pltpu.PrefetchScalarGridSpec(
            num_scalar_prefetch=1,
            grid=(SHARDS // TEAM,),
            in_specs=[pl.BlockSpec(memory_space=pltpu.VMEM)] * DEPTH,
            out_specs=pl.BlockSpec((TEAM, ROWS, WIDTH), lambda i, table: (i, 0, 0)),
        ),
        compiler_params=params(),
        cost_estimate=cost(0, 4 * SHARDS * ROWS * WIDTH),
        name="mean_out",
    )(table, *chunks)


STEPS = 4
STRIP = WIDTH // STEPS
LONG = WIDTH // 2


def precond_body(table, mean, left, right, out, roots, middle, scaled, sums, sems):
    slot = table[PICK]
    second = pltpu.make_async_copy(right.at[slot], roots.at[1], sems.at[STEPS])
    first = pltpu.make_async_copy(left.at[slot], roots.at[0], sems.at[STEPS + 1])
    second.start()
    first.start()
    sums[...] = jnp.zeros_like(sums)
    group = LONG // ROWS

    def power(step, unused):
        own = mean[pl.ds(pl.multiple_of(step * STRIP, STRIP), STRIP), :].astype(f32)
        sums[0:1, :] += jnp.sum(own * own, axis=0, keepdims=True)
        return unused

    lax.fori_loop(0, STEPS, power, 0)
    second.wait()

    def apply_right(step, unused):
        rows = pl.ds(pl.multiple_of(step * LONG, LONG), LONG)
        middle[rows, :] = jnp.dot(mean[rows, :], roots[1], preferred_element_type=f32).astype(bf16)
        return unused

    lax.fori_loop(0, WIDTH // LONG, apply_right, 0)
    first.wait()

    def apply_left(step, unused):
        rows = pl.ds(pl.multiple_of(step * LONG, LONG), LONG)
        product = jnp.dot(roots[0, rows, :], middle[...], preferred_element_type=f32).astype(bf16)
        wide = product.astype(f32)
        sums[1:2, :] += jnp.sum(wide * wide, axis=0, keepdims=True)
        scaled[pl.ds(step * group, group)] = product.reshape(group, ROWS, WIDTH)
        return unused

    lax.fori_loop(0, WIDTH // LONG, apply_left, 0)
    grad_power = jnp.sum(sums[0:1, :], axis=1, keepdims=True) * (1.0 / (WIDTH * WIDTH))
    pre_power = jnp.sum(sums[1:2, :], axis=1, keepdims=True) * (1.0 / (WIDTH * WIDTH))
    factor = jnp.sqrt((grad_power + epsilon) / (pre_power + epsilon))
    sends = []
    for step in range(STEPS):
        part = pl.ds(step * TEAM, TEAM)

        def scale(i, unused, step=step):
            scaled[step * TEAM + i] = (scaled[step * TEAM + i].astype(f32) * factor).astype(bf16)
            return unused

        lax.fori_loop(0, TEAM, scale, 0)
        sends.append(pltpu.make_async_copy(scaled.at[part], out.at[part], sems.at[step]))
        sends[-1].start()
    for send in sends:
        send.wait()


def precond(table, mean, left_roots, right_roots):
    anywhere = pl.BlockSpec(memory_space=pl.ANY)
    left_roots = pltpu.with_memory_space_constraint(left_roots, pltpu.HBM)
    right_roots = pltpu.with_memory_space_constraint(right_roots, pltpu.HBM)
    return pl.pallas_call(
        precond_body,
        out_shape=pltpu.HBM((SHARDS, ROWS, WIDTH), bf16),
        in_specs=[
            pl.BlockSpec(memory_space=pltpu.SMEM),
            pl.BlockSpec(memory_space=pltpu.VMEM),
            anywhere,
            anywhere,
        ],
        out_specs=anywhere,
        scratch_shapes=[
            pltpu.VMEM((2, WIDTH, WIDTH), bf16),
            pltpu.VMEM((WIDTH, WIDTH), bf16),
            pltpu.VMEM((SHARDS, ROWS, WIDTH), bf16),
            pltpu.VMEM((8, WIDTH), f32),
            pltpu.SemaphoreType.DMA((STEPS + 2,)),
        ],
        compiler_params=params(),
        cost_estimate=cost(80 * WIDTH**3, 8 * WIDTH**2),
        name="precond",
    )(table, mean, left_roots, right_roots)


def gram_body(grads, out, whole, terms, sems):
    scale = 1.0 / (WIDTH * DEPTH * CORES)
    per = STRIP // CHUNK
    for rep in range(CORES):
        whole[rep] = grads[:, rep].reshape(WIDTH, WIDTH)
    sends = []
    for step in range(STEPS):
        here = slice(step * STRIP, (step + 1) * STRIP)
        rest = slice(step * STRIP, WIDTH)
        left = right = None
        for rep in range(CORES):
            first = lax.dot_general(
                whole[rep, here, :], whole[rep, rest, :], (((1,), (1,)), ((), ())), preferred_element_type=f32
            )
            second = lax.dot_general(
                whole[rep, :, here], whole[rep, :, rest], (((0,), (0,)), ((), ())), preferred_element_type=f32
            )
            left = first if left is None else left + first
            right = second if right is None else right + second
        for side, value in enumerate((left, right)):
            value = value * scale
            terms[step * per : (step + 1) * per, side, :, rest] = value.astype(bf16).reshape(per, CHUNK, -1)
            for other in range(step + 1, STEPS):
                offset = (other - step) * STRIP
                cell = value[:, offset : offset + STRIP].T.astype(bf16).reshape(per, CHUNK, STRIP)
                terms[other * per : (other + 1) * per, side, :, here] = cell
        part = pl.ds(step * per, per)
        sends.append(pltpu.make_async_copy(terms.at[part], out.at[part], sems.at[step]))
        sends[-1].start()
    for send in sends:
        send.wait()


def gram(grads):
    return pl.pallas_call(
        gram_body,
        out_shape=pltpu.HBM((DEPTH, 2, CHUNK, WIDTH), bf16),
        in_specs=[pl.BlockSpec(memory_space=pltpu.VMEM)],
        out_specs=pl.BlockSpec(memory_space=pl.ANY),
        scratch_shapes=[
            pltpu.VMEM((CORES, WIDTH, WIDTH), bf16),
            pltpu.VMEM((DEPTH, 2, CHUNK, WIDTH), bf16),
            pltpu.SemaphoreType.DMA((STEPS,)),
        ],
        compiler_params=params(),
        cost_estimate=cost(8 * WIDTH**3, 8 * WIDTH**2),
        name="gram",
    )(grads)


GROUP = 6


def finish_body(table, returned, swapped, share, other, direction, statistics):
    core = lax.axis_index("core")
    step = pl.program_id(0)
    for i in range(GROUP):
        kind, owner = table[KIND + GROUP * step + i], table[OWNER + GROUP * step + i]

        @pl.when(kind == core)
        def _():
            direction[i] = returned[owner]

        @pl.when(kind != core)
        def _():
            direction[i] = swapped[owner]

    @pl.when(step == 0)
    def _():
        rows = pl.ds(pl.multiple_of(core * ROWS, ROWS), ROWS)
        for slot in range(SLOTS):
            for side in range(2):
                kept = share[side, rows, :].astype(f32)
                got = other[side, rows, :].astype(f32)
                value = jnp.where(table[SLOTKIND + slot] == core, kept, got)
                statistics[slot, side] = jnp.where(table[FILLED + slot] == 1, value, 0.0)


def finish(table, returned, swapped, share, other):
    return pl.pallas_call(
        finish_body,
        out_shape=(
            jax.ShapeDtypeStruct((BLOCKS, ROWS, WIDTH), bf16),
            jax.ShapeDtypeStruct((SLOTS, 2, ROWS, WIDTH), f32),
        ),
        grid_spec=pltpu.PrefetchScalarGridSpec(
            num_scalar_prefetch=1,
            grid=(BLOCKS // GROUP,),
            in_specs=[pl.BlockSpec(memory_space=pltpu.VMEM)] * 4,
            out_specs=(
                pl.BlockSpec((GROUP, ROWS, WIDTH), lambda i, table: (i, 0, 0)),
                pl.BlockSpec((SLOTS, 2, ROWS, WIDTH), lambda i, table: (0, 0, 0, 0)),
            ),
        ),
        compiler_params=params(),
        cost_estimate=cost(0, 24 * BLOCKS * ROWS * WIDTH),
        name="finish",
    )(table, returned, swapped, share, other)


def local(grads, assignment, piece_slot, left_roots, right_roots):
    swap = functools.partial(lax.ppermute, axis_name="core", perm=[(0, 1), (1, 0)])
    exchange = functools.partial(lax.all_to_all, axis_name="shard", split_axis=0, concat_axis=0, tiled=True)

    def along(array, shift):
        return lax.ppermute(array, "z", [(z, (z + shift) % DEPTH) for z in range(DEPTH)])

    pieces = grads.reshape(BLOCKS, ROWS, WIDTH)
    table, outgoing = front(assignment, piece_slot, pieces)
    table = pltpu.with_memory_space_constraint(table, pltpu.HBM)
    other = swap(outgoing)

    sums = pair_sum(table, pieces, other)
    parts = [sums[0]] + [along(sums[shift], shift) for shift in ORDER]
    owned = exchange(route(table, other, route(table, pieces)))
    chunk = mean_of(parts)
    chunks = {0: chunk} | {shift: along(chunk, shift) for shift in (2, 6, 1, 7)}
    chunks |= {4: along(chunks[2], 2), 3: along(chunks[2], 1), 5: along(chunks[6], 7)}
    chunks = [chunks[shift] for shift in HOPS]
    packed, owned = lax.optimization_barrier((mean_out(table, chunks), owned))
    mean = exchange(packed).reshape(WIDTH, WIDTH)

    terms = gram(owned)
    mean, unused = lax.optimization_barrier((mean, terms))
    share = lax.psum_scatter(terms.reshape(DEPTH * 2 * CHUNK, WIDTH), "z", scatter_dimension=0, tiled=True)
    share = share.reshape(2, CHUNK, WIDTH)

    returned = exchange(precond(table, mean, left_roots, right_roots))
    direction, statistics = finish(table, returned, swap(returned), share, swap(share))
    return statistics, direction.reshape(BLOCKS * ROWS, WIDTH)


def solution(mesh):
    fine = Mesh(mesh.devices.reshape(SHARDS, DEPTH, CORES), ("shard", "z", "core"))
    roots = P("shard", None, None)
    return jax.shard_map(
        local,
        mesh=fine,
        in_specs=(P(("z", "core"), "shard", None), P(), P(), roots, roots),
        out_specs=(P("shard", None, ("z", "core"), None), P("shard", None)),
        check_vma=False,
    )
```

```python
import functools

import jax
import jax.numpy as jnp
from jax import lax
from jax.experimental import pallas as pl
from jax.experimental.pallas import tpu as pltpu
from jax.sharding import Mesh, PartitionSpec as P

epsilon = 1e-06
f32 = jnp.float32
bf16 = jnp.bfloat16

SHARDS, DEPTH, CORES = 16, 8, 2
SLOTS, BLOCKS, ROWS, WIDTH = 2, 18, 64, 1024
HALF = BLOCKS // CORES
CHUNK = WIDTH // DEPTH

ORDER = (4, 3, 5, 2, 6, 1, 7)
HOPS = (0, 2, 6, 1, 7, 4, 3, 5)
DIRECT = 5

OWN, SEND, PLACE, KIND, OWNER, FILLED, SLOTKIND, PICK, COLUMN = 0, 9, 18, 34, 52, 70, 72, 74, 75
USED, SIZE = 75, 128


def params(megabytes=32):
    return pltpu.CompilerParams(vmem_limit_bytes=megabytes * 1024 * 1024)


def cost(flops, moved):
    return pl.CostEstimate(flops=flops, bytes_accessed=moved, transcendentals=0)


def front_body(assignment, piece_slot, pieces, table, out, held, sem):
    shard, core = lax.axis_index("shard"), lax.axis_index("core")
    fetch = pltpu.make_async_copy(pieces, held, sem)
    fetch.start()

    for i in (*range(PLACE, PLACE + SHARDS), *range(FILLED, USED)):
        table[i] = 0
    for i, shift in enumerate(HOPS):
        table[COLUMN + i] = lax.rem(lax.axis_index("z") + DEPTH - shift, DEPTH)
    slots = [assignment[k] for k in range(BLOCKS)]

    def block(k, unused):
        slot, place = assignment[k], piece_slot[k]
        rank = jnp.int32(0)
        for other in slots:
            rank += jnp.where(other < slot, 1, 0)
        kind, index = lax.rem(rank, CORES), lax.div(rank, CORES)
        owner, which = lax.div(slot, SLOTS), lax.rem(slot, SLOTS)
        table[jnp.where(kind == core, OWN, SEND) + index] = place
        table[KIND + place] = kind
        table[OWNER + place] = owner

        @pl.when(kind == core)
        def _():
            table[PLACE + owner] = index

        @pl.when(owner == shard)
        def _():
            table[FILLED + which] = 1
            table[SLOTKIND + which] = kind

        @pl.when((owner == shard) & (kind == core))
        def _():
            table[PICK] = which

        return unused

    lax.fori_loop(0, BLOCKS, block, 0)
    fetch.wait()
    for n in range(HALF):
        out[n] = held[table[SEND + n]]


def front(assignment, piece_slot, pieces):
    smem = pl.BlockSpec(memory_space=pltpu.SMEM)
    return pl.pallas_call(
        front_body,
        out_shape=(
            pltpu.HBM((SIZE,), jnp.int32),
            pltpu.VMEM((HALF, ROWS, WIDTH), bf16),
        ),
        in_specs=[smem, smem, pl.BlockSpec(memory_space=pl.ANY)],
        out_specs=(smem, pl.BlockSpec(memory_space=pltpu.VMEM)),
        scratch_shapes=[pltpu.VMEM((BLOCKS, ROWS, WIDTH), bf16), pltpu.SemaphoreType.DMA],
        compiler_params=params(56),
        cost_estimate=cost(0, 6 * BLOCKS * ROWS * WIDTH),
        name="front",
    )(assignment, piece_slot, pieces)


def pair_sum_body(table, pieces, other, *rest):
    sums, held = rest[:-1], rest[-1]
    me = lax.axis_index("z")

    def add(n, unused):
        held[...] = (pieces[table[OWN + n]].astype(f32) + other[n].astype(f32)).astype(bf16)
        for shift in range(DEPTH):
            target = lax.rem(me + shift, DEPTH)
            sums[shift][n] = held[:, pl.ds(pl.multiple_of(target * CHUNK, CHUNK), CHUNK)]
        return unused

    lax.fori_loop(0, HALF, add, 0)


def pair_sum(table, pieces, other):
    vmem = pl.BlockSpec(memory_space=pltpu.VMEM)
    return pl.pallas_call(
        pair_sum_body,
        out_shape=[jax.ShapeDtypeStruct((HALF, ROWS, CHUNK), bf16)] * DEPTH,
        in_specs=[pl.BlockSpec(memory_space=pltpu.SMEM), vmem, vmem],
        out_specs=[vmem] * DEPTH,
        scratch_shapes=[pltpu.VMEM((ROWS, WIDTH), bf16)],
        compiler_params=params(),
        cost_estimate=cost(HALF * ROWS * WIDTH, 6 * HALF * ROWS * WIDTH),
        name="pair_sum",
    )(table, pieces, other)


TEAM = 4
LOAD = 8


def route_own_body(table, pieces, routed):
    step = pl.program_id(0)
    for i in range(LOAD):
        routed[i, 0] = pieces[table[OWN + table[PLACE + LOAD * step + i]]]


def route_other_body(table, other, half, routed):
    step = pl.program_id(0)
    for i in range(LOAD):
        routed[i, 0] = other[table[PLACE + LOAD * step + i]]


def route(table, source, half=None):
    part = 0 if half is None else 1
    block = pl.BlockSpec((LOAD, 1, ROWS, WIDTH), lambda i, table: (i, part, 0, 0))
    return pl.pallas_call(
        route_other_body if part else route_own_body,
        out_shape=pltpu.HBM((SHARDS, CORES, ROWS, WIDTH), bf16),
        grid_spec=pltpu.PrefetchScalarGridSpec(
            num_scalar_prefetch=1,
            grid=(SHARDS // LOAD,),
            in_specs=[pl.BlockSpec(memory_space=pltpu.VMEM)] + [pl.BlockSpec(memory_space=pl.ANY)] * part,
            out_specs=block,
        ),
        input_output_aliases={2: 0} if part else {},
        compiler_params=params(),
        cost_estimate=cost(0, 4 * SHARDS * ROWS * WIDTH),
        name="route_other" if part else "route_own",
    )(table, source, *([half] if part else []))


def mean_body(*refs):
    parts, out = refs[:-1], refs[-1]
    for n in range(HALF):
        total = parts[0][n].astype(f32)
        for part in parts[1:]:
            total += part[n].astype(f32)
        out[n] = (total * (1.0 / (DEPTH * CORES))).astype(bf16)


def mean_of(parts):
    vmem = pl.BlockSpec(memory_space=pltpu.VMEM)
    return pl.pallas_call(
        mean_body,
        out_shape=jax.ShapeDtypeStruct((HALF, ROWS, CHUNK), bf16),
        in_specs=[vmem] * DEPTH,
        out_specs=vmem,
        compiler_params=params(),
        cost_estimate=cost(DEPTH * HALF * ROWS * CHUNK, 18 * HALF * ROWS * CHUNK),
        name="mean",
    )(*parts)


def mean_out_body(table, *refs, count):
    chunks, out = refs[:count], refs[-1]
    for i, chunk in enumerate(chunks):

        @pl.when(pl.program_id(0) == i)
        def _(chunk=chunk):
            for owner in range(SHARDS):
                out[owner] = chunk[table[PLACE + owner]]


def mean_out(table, chunks, half=None):
    first, extra = (0, 0) if half is None else (DIRECT, 1)
    count = len(chunks)
    vmem, anywhere = pl.BlockSpec(memory_space=pltpu.VMEM), pl.BlockSpec(memory_space=pl.ANY)
    return pl.pallas_call(
        functools.partial(mean_out_body, count=count),
        out_shape=pltpu.HBM((SHARDS, ROWS, WIDTH), bf16),
        grid_spec=pltpu.PrefetchScalarGridSpec(
            num_scalar_prefetch=1,
            grid=(count,),
            in_specs=[vmem] * count + [anywhere] * extra,
            out_specs=pl.BlockSpec((SHARDS, ROWS, CHUNK), lambda i, table: (0, 0, table[COLUMN + first + i])),
        ),
        input_output_aliases={1 + count: 0} if extra else {},
        compiler_params=params(),
        cost_estimate=cost(0, 4 * SHARDS * ROWS * CHUNK * count),
        name="mean_late" if extra else "mean_early",
    )(table, *chunks, *([half] if extra else []))


STEPS = 4
STRIP = WIDTH // STEPS
LONG = WIDTH // 2


def precond_body(table, mean, left, right, out, roots, middle, scaled, sums, sems):
    slot = table[PICK]
    second = pltpu.make_async_copy(right.at[slot], roots.at[1], sems.at[STEPS])
    first = pltpu.make_async_copy(left.at[slot], roots.at[0], sems.at[STEPS + 1])
    second.start()
    first.start()
    sums[...] = jnp.zeros_like(sums)
    group = LONG // ROWS

    def power(step, unused):
        own = mean[pl.ds(pl.multiple_of(step * STRIP, STRIP), STRIP), :].astype(f32)
        sums[0:1, :] += jnp.sum(own * own, axis=0, keepdims=True)
        return unused

    lax.fori_loop(0, STEPS, power, 0)
    second.wait()

    def apply_right(step, unused):
        rows = pl.ds(pl.multiple_of(step * LONG, LONG), LONG)
        middle[rows, :] = jnp.dot(mean[rows, :], roots[1], preferred_element_type=f32).astype(bf16)
        return unused

    lax.fori_loop(0, WIDTH // LONG, apply_right, 0)
    first.wait()

    def apply_left(step, unused):
        rows = pl.ds(pl.multiple_of(step * LONG, LONG), LONG)
        product = jnp.dot(roots[0, rows, :], middle[...], preferred_element_type=f32).astype(bf16)
        wide = product.astype(f32)
        sums[1:2, :] += jnp.sum(wide * wide, axis=0, keepdims=True)
        scaled[pl.ds(step * group, group)] = product.reshape(group, ROWS, WIDTH)
        return unused

    lax.fori_loop(0, WIDTH // LONG, apply_left, 0)
    grad_power = jnp.sum(sums[0:1, :], axis=1, keepdims=True) * (1.0 / (WIDTH * WIDTH))
    pre_power = jnp.sum(sums[1:2, :], axis=1, keepdims=True) * (1.0 / (WIDTH * WIDTH))
    factor = jnp.sqrt((grad_power + epsilon) / (pre_power + epsilon))
    sends = []
    for step in range(STEPS):
        part = pl.ds(step * TEAM, TEAM)

        def scale(i, unused, step=step):
            scaled[step * TEAM + i] = (scaled[step * TEAM + i].astype(f32) * factor).astype(bf16)
            return unused

        lax.fori_loop(0, TEAM, scale, 0)
        sends.append(pltpu.make_async_copy(scaled.at[part], out.at[part], sems.at[step]))
        sends[-1].start()
    for send in sends:
        send.wait()


def precond(table, mean, left_roots, right_roots):
    anywhere = pl.BlockSpec(memory_space=pl.ANY)
    left_roots = pltpu.with_memory_space_constraint(left_roots, pltpu.HBM)
    right_roots = pltpu.with_memory_space_constraint(right_roots, pltpu.HBM)
    return pl.pallas_call(
        precond_body,
        out_shape=pltpu.HBM((SHARDS, ROWS, WIDTH), bf16),
        in_specs=[
            pl.BlockSpec(memory_space=pltpu.SMEM),
            pl.BlockSpec(memory_space=pltpu.VMEM),
            anywhere,
            anywhere,
        ],
        out_specs=anywhere,
        scratch_shapes=[
            pltpu.VMEM((2, WIDTH, WIDTH), bf16),
            pltpu.VMEM((WIDTH, WIDTH), bf16),
            pltpu.VMEM((SHARDS, ROWS, WIDTH), bf16),
            pltpu.VMEM((8, WIDTH), f32),
            pltpu.SemaphoreType.DMA((STEPS + 2,)),
        ],
        compiler_params=params(),
        cost_estimate=cost(80 * WIDTH**3, 8 * WIDTH**2),
        name="precond",
    )(table, mean, left_roots, right_roots)


def gram_body(grads, out, whole, terms, sems):
    scale = 1.0 / (WIDTH * DEPTH * CORES)
    per = STRIP // CHUNK
    for rep in range(CORES):
        whole[rep] = grads[:, rep].reshape(WIDTH, WIDTH)
    sends = []
    for step in range(STEPS):
        here = slice(step * STRIP, (step + 1) * STRIP)
        rest = slice(step * STRIP, WIDTH)
        left = right = None
        for rep in range(CORES):
            first = lax.dot_general(
                whole[rep, here, :], whole[rep, rest, :], (((1,), (1,)), ((), ())), preferred_element_type=f32
            )
            second = lax.dot_general(
                whole[rep, :, here], whole[rep, :, rest], (((0,), (0,)), ((), ())), preferred_element_type=f32
            )
            left = first if left is None else left + first
            right = second if right is None else right + second
        for side, value in enumerate((left, right)):
            value = value * scale
            terms[step * per : (step + 1) * per, side, :, rest] = value.astype(bf16).reshape(per, CHUNK, -1)
            for other in range(step + 1, STEPS):
                offset = (other - step) * STRIP
                cell = value[:, offset : offset + STRIP].T.astype(bf16).reshape(per, CHUNK, STRIP)
                terms[other * per : (other + 1) * per, side, :, here] = cell
        part = pl.ds(step * per, per)
        sends.append(pltpu.make_async_copy(terms.at[part], out.at[part], sems.at[step]))
        sends[-1].start()
    for send in sends:
        send.wait()


def gram(grads):
    return pl.pallas_call(
        gram_body,
        out_shape=pltpu.HBM((DEPTH, 2, CHUNK, WIDTH), bf16),
        in_specs=[pl.BlockSpec(memory_space=pltpu.VMEM)],
        out_specs=pl.BlockSpec(memory_space=pl.ANY),
        scratch_shapes=[
            pltpu.VMEM((CORES, WIDTH, WIDTH), bf16),
            pltpu.VMEM((DEPTH, 2, CHUNK, WIDTH), bf16),
            pltpu.SemaphoreType.DMA((STEPS,)),
        ],
        compiler_params=params(),
        cost_estimate=cost(8 * WIDTH**3, 8 * WIDTH**2),
        name="gram",
    )(grads)


GROUP = 6


def finish_body(table, returned, swapped, share, other, direction, statistics):
    core = lax.axis_index("core")
    step = pl.program_id(0)
    for i in range(GROUP):
        kind, owner = table[KIND + GROUP * step + i], table[OWNER + GROUP * step + i]

        @pl.when(kind == core)
        def _():
            direction[i] = returned[owner]

        @pl.when(kind != core)
        def _():
            direction[i] = swapped[owner]

    @pl.when(step == 0)
    def _():
        rows = pl.ds(pl.multiple_of(core * ROWS, ROWS), ROWS)
        for slot in range(SLOTS):
            for side in range(2):
                kept = share[side, rows, :].astype(f32)
                got = other[side, rows, :].astype(f32)
                value = jnp.where(table[SLOTKIND + slot] == core, kept, got)
                statistics[slot, side] = jnp.where(table[FILLED + slot] == 1, value, 0.0)


def finish(table, returned, swapped, share, other):
    return pl.pallas_call(
        finish_body,
        out_shape=(
            jax.ShapeDtypeStruct((BLOCKS, ROWS, WIDTH), bf16),
            jax.ShapeDtypeStruct((SLOTS, 2, ROWS, WIDTH), f32),
        ),
        grid_spec=pltpu.PrefetchScalarGridSpec(
            num_scalar_prefetch=1,
            grid=(BLOCKS // GROUP,),
            in_specs=[pl.BlockSpec(memory_space=pltpu.VMEM)] * 4,
            out_specs=(
                pl.BlockSpec((GROUP, ROWS, WIDTH), lambda i, table: (i, 0, 0)),
                pl.BlockSpec((SLOTS, 2, ROWS, WIDTH), lambda i, table: (0, 0, 0, 0)),
            ),
        ),
        compiler_params=params(),
        cost_estimate=cost(0, 24 * BLOCKS * ROWS * WIDTH),
        name="finish",
    )(table, returned, swapped, share, other)


def local(grads, assignment, piece_slot, left_roots, right_roots):
    swap = functools.partial(lax.ppermute, axis_name="core", perm=[(0, 1), (1, 0)])
    exchange = functools.partial(lax.all_to_all, axis_name="shard", split_axis=0, concat_axis=0, tiled=True)

    def along(array, shift):
        return lax.ppermute(array, "z", [(z, (z + shift) % DEPTH) for z in range(DEPTH)])

    pieces = grads.reshape(BLOCKS, ROWS, WIDTH)
    table, outgoing = front(assignment, piece_slot, pieces)
    table = pltpu.with_memory_space_constraint(table, pltpu.HBM)
    other = swap(outgoing)

    sums = pair_sum(table, pieces, other)
    parts = [sums[0]] + [along(sums[shift], shift) for shift in ORDER]
    owned = exchange(route(table, other, route(table, pieces)))
    chunk = mean_of(parts)
    chunks = {0: chunk} | {shift: along(chunk, shift) for shift in (2, 6, 1, 7)}
    chunks |= {4: along(chunks[2], 2), 3: along(chunks[2], 1), 5: along(chunks[6], 7)}
    chunks = [chunks[shift] for shift in HOPS]
    packed = mean_out(table, chunks[DIRECT:], mean_out(table, chunks[:DIRECT]))
    packed, owned = lax.optimization_barrier((packed, owned))
    mean = exchange(packed).reshape(WIDTH, WIDTH)

    terms = gram(owned)
    mean, unused = lax.optimization_barrier((mean, terms))
    share = lax.psum_scatter(terms.reshape(DEPTH * 2 * CHUNK, WIDTH), "z", scatter_dimension=0, tiled=True)
    share = share.reshape(2, CHUNK, WIDTH)

    returned = exchange(precond(table, mean, left_roots, right_roots))
    direction, statistics = finish(table, returned, swap(returned), share, swap(share))
    return statistics, direction.reshape(BLOCKS * ROWS, WIDTH)


def solution(mesh):
    fine = Mesh(mesh.devices.reshape(SHARDS, DEPTH, CORES), ("shard", "z", "core"))
    roots = P("shard", None, None)
    return jax.shard_map(
        local,
        mesh=fine,
        in_specs=(P(("z", "core"), "shard", None), P(), P(), roots, roots),
        out_specs=(P("shard", None, ("z", "core"), None), P("shard", None)),
        check_vma=False,
    )
```

```python
import functools

import jax
import jax.numpy as jnp
from jax import lax
from jax.experimental import pallas as pl
from jax.experimental.pallas import tpu as pltpu
from jax.sharding import Mesh, PartitionSpec as P

epsilon = 1e-06
f32 = jnp.float32
bf16 = jnp.bfloat16

SHARDS, DEPTH, CORES = 16, 8, 2
SLOTS, BLOCKS, ROWS, WIDTH = 2, 18, 64, 1024
HALF = BLOCKS // CORES
CHUNK = WIDTH // DEPTH

ORDER = (4, 3, 5, 2, 6, 1, 7)
HOPS = (2, 6, 1, 7, 4, 3, 5, 0)

OWN, SEND, PLACE, KIND, OWNER, FILLED, SLOTKIND, PICK, USED, SIZE = 0, 9, 18, 34, 52, 70, 72, 74, 75, 128


def params(megabytes=32):
    return pltpu.CompilerParams(vmem_limit_bytes=megabytes * 1024 * 1024)


def cost(flops, moved):
    return pl.CostEstimate(flops=flops, bytes_accessed=moved, transcendentals=0)


def front_body(assignment, piece_slot, pieces, table, out, held, sem):
    shard, core = lax.axis_index("shard"), lax.axis_index("core")
    fetch = pltpu.make_async_copy(pieces, held, sem)
    fetch.start()

    for i in (*range(PLACE, PLACE + SHARDS), *range(FILLED, USED)):
        table[i] = 0
    slots = [assignment[k] for k in range(BLOCKS)]

    def block(k, unused):
        slot, place = assignment[k], piece_slot[k]
        rank = jnp.int32(0)
        for other in slots:
            rank += jnp.where(other < slot, 1, 0)
        kind, index = lax.rem(rank, CORES), lax.div(rank, CORES)
        owner, which = lax.div(slot, SLOTS), lax.rem(slot, SLOTS)
        table[jnp.where(kind == core, OWN, SEND) + index] = place
        table[KIND + place] = kind
        table[OWNER + place] = owner

        @pl.when(kind == core)
        def _():
            table[PLACE + owner] = index

        @pl.when(owner == shard)
        def _():
            table[FILLED + which] = 1
            table[SLOTKIND + which] = kind

        @pl.when((owner == shard) & (kind == core))
        def _():
            table[PICK] = which

        return unused

    lax.fori_loop(0, BLOCKS, block, 0)
    fetch.wait()
    for n in range(HALF):
        out[n] = held[table[SEND + n]]


def front(assignment, piece_slot, pieces):
    smem = pl.BlockSpec(memory_space=pltpu.SMEM)
    return pl.pallas_call(
        front_body,
        out_shape=(
            pltpu.HBM((SIZE,), jnp.int32),
            pltpu.VMEM((HALF, ROWS, WIDTH), bf16),
        ),
        in_specs=[smem, smem, pl.BlockSpec(memory_space=pl.ANY)],
        out_specs=(smem, pl.BlockSpec(memory_space=pltpu.VMEM)),
        scratch_shapes=[pltpu.VMEM((BLOCKS, ROWS, WIDTH), bf16), pltpu.SemaphoreType.DMA],
        compiler_params=params(56),
        cost_estimate=cost(0, 6 * BLOCKS * ROWS * WIDTH),
        name="front",
    )(assignment, piece_slot, pieces)


def pair_sum_body(table, pieces, other, *rest):
    sums, held = rest[:-1], rest[-1]
    me = lax.axis_index("z")

    def add(n, unused):
        held[...] = (pieces[table[OWN + n]].astype(f32) + other[n].astype(f32)).astype(bf16)
        for shift in range(DEPTH):
            target = lax.rem(me + shift, DEPTH)
            sums[shift][n] = held[:, pl.ds(pl.multiple_of(target * CHUNK, CHUNK), CHUNK)]
        return unused

    lax.fori_loop(0, HALF, add, 0)


def pair_sum(table, pieces, other):
    vmem = pl.BlockSpec(memory_space=pltpu.VMEM)
    return pl.pallas_call(
        pair_sum_body,
        out_shape=[jax.ShapeDtypeStruct((HALF, ROWS, CHUNK), bf16)] * DEPTH,
        in_specs=[pl.BlockSpec(memory_space=pltpu.SMEM), vmem, vmem],
        out_specs=[vmem] * DEPTH,
        scratch_shapes=[pltpu.VMEM((ROWS, WIDTH), bf16)],
        compiler_params=params(),
        cost_estimate=cost(HALF * ROWS * WIDTH, 6 * HALF * ROWS * WIDTH),
        name="pair_sum",
    )(table, pieces, other)


TEAM = 4
LOAD = 8


def route_own_body(table, pieces, routed):
    step = pl.program_id(0)
    for i in range(LOAD):
        routed[i, 0] = pieces[table[OWN + table[PLACE + LOAD * step + i]]]


def route_other_body(table, other, half, routed):
    step = pl.program_id(0)
    for i in range(LOAD):
        routed[i, 0] = other[table[PLACE + LOAD * step + i]]


def route(table, source, half=None):
    part = 0 if half is None else 1
    block = pl.BlockSpec((LOAD, 1, ROWS, WIDTH), lambda i, table: (i, part, 0, 0))
    return pl.pallas_call(
        route_other_body if part else route_own_body,
        out_shape=pltpu.HBM((SHARDS, CORES, ROWS, WIDTH), bf16),
        grid_spec=pltpu.PrefetchScalarGridSpec(
            num_scalar_prefetch=1,
            grid=(SHARDS // LOAD,),
            in_specs=[pl.BlockSpec(memory_space=pltpu.VMEM)] + [pl.BlockSpec(memory_space=pl.ANY)] * part,
            out_specs=block,
        ),
        input_output_aliases={2: 0} if part else {},
        compiler_params=params(),
        cost_estimate=cost(0, 4 * SHARDS * ROWS * WIDTH),
        name="route_other" if part else "route_own",
    )(table, source, *([half] if part else []))


def mean_body(*refs):
    parts, out = refs[:-1], refs[-1]
    for n in range(HALF):
        total = parts[0][n].astype(f32)
        for part in parts[1:]:
            total += part[n].astype(f32)
        out[n] = (total * (1.0 / (DEPTH * CORES))).astype(bf16)


def mean_of(parts):
    vmem = pl.BlockSpec(memory_space=pltpu.VMEM)
    return pl.pallas_call(
        mean_body,
        out_shape=jax.ShapeDtypeStruct((HALF, ROWS, CHUNK), bf16),
        in_specs=[vmem] * DEPTH,
        out_specs=vmem,
        compiler_params=params(),
        cost_estimate=cost(DEPTH * HALF * ROWS * CHUNK, 18 * HALF * ROWS * CHUNK),
        name="mean",
    )(*parts)


def mean_out_body(table, *refs):
    chunks, out = refs[:-1], refs[-1]
    me, step = lax.axis_index("z"), pl.program_id(0)

    def one(i, unused):
        index = table[PLACE + TEAM * step + i]
        for shift, chunk in zip(HOPS, chunks):
            source = lax.rem(me + DEPTH - shift, DEPTH)
            columns = pl.ds(pl.multiple_of(source * CHUNK, CHUNK), CHUNK)
            out[i, :, columns] = chunk[index]
        return unused

    lax.fori_loop(0, TEAM, one, 0)


def mean_out(table, chunks):
    return pl.pallas_call(
        mean_out_body,
        out_shape=pltpu.HBM((SHARDS, ROWS, WIDTH), bf16),
        grid_spec=pltpu.PrefetchScalarGridSpec(
            num_scalar_prefetch=1,
            grid=(SHARDS // TEAM,),
            in_specs=[pl.BlockSpec(memory_space=pltpu.VMEM)] * DEPTH,
            out_specs=pl.BlockSpec((TEAM, ROWS, WIDTH), lambda i, table: (i, 0, 0)),
        ),
        compiler_params=params(),
        cost_estimate=cost(0, 4 * SHARDS * ROWS * WIDTH),
        name="mean_out",
    )(table, *chunks)


STEPS = 4
STRIP = WIDTH // STEPS
LONG = WIDTH // 2


def precond_body(table, mean, left, right, out, roots, middle, scaled, sums, sems):
    slot = table[PICK]
    second = pltpu.make_async_copy(right.at[slot], roots.at[1], sems.at[STEPS])
    first = pltpu.make_async_copy(left.at[slot], roots.at[0], sems.at[STEPS + 1])
    second.start()
    first.start()
    sums[...] = jnp.zeros_like(sums)
    group = LONG // ROWS

    def power(step, unused):
        own = mean[pl.ds(pl.multiple_of(step * STRIP, STRIP), STRIP), :].astype(f32)
        sums[0:1, :] += jnp.sum(own * own, axis=0, keepdims=True)
        return unused

    lax.fori_loop(0, STEPS, power, 0)
    second.wait()

    def apply_right(step, unused):
        rows = pl.ds(pl.multiple_of(step * LONG, LONG), LONG)
        middle[rows, :] = jnp.dot(mean[rows, :], roots[1], preferred_element_type=f32).astype(bf16)
        return unused

    lax.fori_loop(0, WIDTH // LONG, apply_right, 0)
    first.wait()

    def apply_left(step, unused):
        rows = pl.ds(pl.multiple_of(step * LONG, LONG), LONG)
        product = jnp.dot(roots[0, rows, :], middle[...], preferred_element_type=f32).astype(bf16)
        wide = product.astype(f32)
        sums[1:2, :] += jnp.sum(wide * wide, axis=0, keepdims=True)
        scaled[pl.ds(step * group, group)] = product.reshape(group, ROWS, WIDTH)
        return unused

    lax.fori_loop(0, WIDTH // LONG, apply_left, 0)
    grad_power = jnp.sum(sums[0:1, :], axis=1, keepdims=True) * (1.0 / (WIDTH * WIDTH))
    pre_power = jnp.sum(sums[1:2, :], axis=1, keepdims=True) * (1.0 / (WIDTH * WIDTH))
    factor = jnp.sqrt((grad_power + epsilon) / (pre_power + epsilon))
    sends = []
    for step in range(STEPS):
        part = pl.ds(step * TEAM, TEAM)

        def scale(i, unused, step=step):
            scaled[step * TEAM + i] = (scaled[step * TEAM + i].astype(f32) * factor).astype(bf16)
            return unused

        lax.fori_loop(0, TEAM, scale, 0)
        sends.append(pltpu.make_async_copy(scaled.at[part], out.at[part], sems.at[step]))
        sends[-1].start()
    for send in sends:
        send.wait()


def precond(table, mean, left_roots, right_roots):
    anywhere = pl.BlockSpec(memory_space=pl.ANY)
    left_roots = pltpu.with_memory_space_constraint(left_roots, pltpu.HBM)
    right_roots = pltpu.with_memory_space_constraint(right_roots, pltpu.HBM)
    return pl.pallas_call(
        precond_body,
        out_shape=pltpu.HBM((SHARDS, ROWS, WIDTH), bf16),
        in_specs=[
            pl.BlockSpec(memory_space=pltpu.SMEM),
            pl.BlockSpec(memory_space=pltpu.VMEM),
            anywhere,
            anywhere,
        ],
        out_specs=anywhere,
        scratch_shapes=[
            pltpu.VMEM((2, WIDTH, WIDTH), bf16),
            pltpu.VMEM((WIDTH, WIDTH), bf16),
            pltpu.VMEM((SHARDS, ROWS, WIDTH), bf16),
            pltpu.VMEM((8, WIDTH), f32),
            pltpu.SemaphoreType.DMA((STEPS + 2,)),
        ],
        compiler_params=params(),
        cost_estimate=cost(80 * WIDTH**3, 8 * WIDTH**2),
        name="precond",
    )(table, mean, left_roots, right_roots)


def gram_body(grads, out, whole, terms, sems):
    scale = 1.0 / (WIDTH * DEPTH * CORES)
    per = STRIP // CHUNK
    for rep in range(CORES):
        whole[rep] = grads[:, rep].reshape(WIDTH, WIDTH)
    sends = []
    for step in range(STEPS):
        here = slice(step * STRIP, (step + 1) * STRIP)
        rest = slice(step * STRIP, WIDTH)
        left = right = None
        for rep in range(CORES):
            first = lax.dot_general(
                whole[rep, here, :], whole[rep, rest, :], (((1,), (1,)), ((), ())), preferred_element_type=f32
            )
            second = lax.dot_general(
                whole[rep, :, here], whole[rep, :, rest], (((0,), (0,)), ((), ())), preferred_element_type=f32
            )
            left = first if left is None else left + first
            right = second if right is None else right + second
        for side, value in enumerate((left, right)):
            value = value * scale
            terms[step * per : (step + 1) * per, side, :, rest] = value.astype(bf16).reshape(per, CHUNK, -1)
            for other in range(step + 1, STEPS):
                offset = (other - step) * STRIP
                cell = value[:, offset : offset + STRIP].T.astype(bf16).reshape(per, CHUNK, STRIP)
                terms[other * per : (other + 1) * per, side, :, here] = cell
        part = pl.ds(step * per, per)
        sends.append(pltpu.make_async_copy(terms.at[part], out.at[part], sems.at[step]))
        sends[-1].start()
    for send in sends:
        send.wait()


def gram(grads):
    return pl.pallas_call(
        gram_body,
        out_shape=pltpu.HBM((DEPTH, 2, CHUNK, WIDTH), bf16),
        in_specs=[pl.BlockSpec(memory_space=pltpu.VMEM)],
        out_specs=pl.BlockSpec(memory_space=pl.ANY),
        scratch_shapes=[
            pltpu.VMEM((CORES, WIDTH, WIDTH), bf16),
            pltpu.VMEM((DEPTH, 2, CHUNK, WIDTH), bf16),
            pltpu.SemaphoreType.DMA((STEPS,)),
        ],
        compiler_params=params(),
        cost_estimate=cost(8 * WIDTH**3, 8 * WIDTH**2),
        name="gram",
    )(grads)


GROUP = 9


def finish_body(table, returned, swapped, share, other, direction, statistics):
    core = lax.axis_index("core")
    step = pl.program_id(0)
    for i in range(GROUP):
        kind, owner = table[KIND + GROUP * step + i], table[OWNER + GROUP * step + i]

        @pl.when(kind == core)
        def _():
            direction[i] = returned[owner]

        @pl.when(kind != core)
        def _():
            direction[i] = swapped[owner]

    @pl.when(step == 0)
    def _():
        rows = pl.ds(pl.multiple_of(core * ROWS, ROWS), ROWS)
        for slot in range(SLOTS):
            for side in range(2):
                kept = share[side, rows, :].astype(f32)
                got = other[side, rows, :].astype(f32)
                value = jnp.where(table[SLOTKIND + slot] == core, kept, got)
                statistics[slot, side] = jnp.where(table[FILLED + slot] == 1, value, 0.0)


def finish(table, returned, swapped, share, other):
    return pl.pallas_call(
        finish_body,
        out_shape=(
            jax.ShapeDtypeStruct((BLOCKS, ROWS, WIDTH), bf16),
            jax.ShapeDtypeStruct((SLOTS, 2, ROWS, WIDTH), f32),
        ),
        grid_spec=pltpu.PrefetchScalarGridSpec(
            num_scalar_prefetch=1,
            grid=(BLOCKS // GROUP,),
            in_specs=[pl.BlockSpec(memory_space=pltpu.VMEM)] * 4,
            out_specs=(
                pl.BlockSpec((GROUP, ROWS, WIDTH), lambda i, table: (i, 0, 0)),
                pl.BlockSpec((SLOTS, 2, ROWS, WIDTH), lambda i, table: (0, 0, 0, 0)),
            ),
        ),
        compiler_params=params(),
        cost_estimate=cost(0, 24 * BLOCKS * ROWS * WIDTH),
        name="finish",
    )(table, returned, swapped, share, other)


def local(grads, assignment, piece_slot, left_roots, right_roots):
    swap = functools.partial(lax.ppermute, axis_name="core", perm=[(0, 1), (1, 0)])
    exchange = functools.partial(lax.all_to_all, axis_name="shard", split_axis=0, concat_axis=0, tiled=True)

    def along(array, shift):
        return lax.ppermute(array, "z", [(z, (z + shift) % DEPTH) for z in range(DEPTH)])

    pieces = grads.reshape(BLOCKS, ROWS, WIDTH)
    table, outgoing = front(assignment, piece_slot, pieces)
    table = pltpu.with_memory_space_constraint(table, pltpu.HBM)
    other = swap(outgoing)

    sums = pair_sum(table, pieces, other)
    parts = [sums[0]] + [along(sums[shift], shift) for shift in ORDER]
    owned = exchange(route(table, other, route(table, pieces)))
    chunk = mean_of(parts)
    chunks = {0: chunk} | {shift: along(chunk, shift) for shift in (2, 6, 1, 7)}
    chunks |= {4: along(chunks[2], 2), 3: along(chunks[2], 1), 5: along(chunks[6], 7)}
    chunks = [chunks[shift] for shift in HOPS]
    packed, owned = lax.optimization_barrier((mean_out(table, chunks), owned))
    mean = exchange(packed).reshape(WIDTH, WIDTH)

    terms = gram(owned)
    mean, unused = lax.optimization_barrier((mean, terms))
    share = lax.psum_scatter(terms.reshape(DEPTH * 2 * CHUNK, WIDTH), "z", scatter_dimension=0, tiled=True)
    share = share.reshape(2, CHUNK, WIDTH)

    returned = exchange(precond(table, mean, left_roots, right_roots))
    direction, statistics = finish(table, returned, swap(returned), share, swap(share))
    return statistics, direction.reshape(BLOCKS * ROWS, WIDTH)


def solution(mesh):
    fine = Mesh(mesh.devices.reshape(SHARDS, DEPTH, CORES), ("shard", "z", "core"))
    roots = P("shard", None, None)
    return jax.shard_map(
        local,
        mesh=fine,
        in_specs=(P(("z", "core"), "shard", None), P(), P(), roots, roots),
        out_specs=(P("shard", None, ("z", "core"), None), P("shard", None)),
        check_vma=False,
    )
```
